512 devices in a mesh: wide: 64 (over y, z_lo, core), narrow: 8 (over x, z_hi).
Axes of the slice: x: 4, y: 8, z: 8 (z_hi: 2, z_lo: 4; z = z_hi * 4 + z_lo), core: 2. Of those that a mesh axis runs over, the one named last changes fastest.
Arguments:
- tokens: bfloat16 [24576, 4096], P('wide', 'narrow'), may hold values from -6 to 6
- grad_out: bfloat16 [24576, 4096], P('wide', 'narrow'), may hold values from -6 to 6
- slot_token: int32 [16384], P('wide'), may hold values from 0 to 383, as said below
- slot_count: int32 [64], P('wide'), may hold values from 64 to 256, as said below
- slot_gate: float32 [16384], P('wide'), may hold values from 0.1 to 1
- w_gate: bfloat16 [4096, 1024], P('wide', 'narrow'), may hold values from -0.09375 to 0.09375
- w_up: bfloat16 [4096, 1024], P('wide', 'narrow'), may hold values from -0.09375 to 0.09375
- w_down: bfloat16 [4096, 1024], P('wide', 'narrow'), may hold values from -0.1875 to 0.1875
Outputs:
- mixed: bfloat16 [24576, 4096], P('wide', 'narrow')
- grad_tokens: bfloat16 [24576, 4096], P('wide', 'narrow')
- grad_gate: float32 [4096, 1024], P('wide', 'narrow')
- grad_up: float32 [4096, 1024], P('wide', 'narrow')
- grad_down: float32 [4096, 1024], P('wide', 'narrow')
The draws below stay inside these ranges and needn't reach their ends.
Inputs may be any that keep to these rules, and one draw needn't show every extreme that they name: `slot_token`: the slots of one index of wide name distinct tokens of that index. `slot_count`: some index of wide fills all 256 slots in every draw.
All inputs are finite; a program needn't handle non-finite values.
Results may differ from the reference program's by a relative error of at most 0.017.
Values may be sent and summed in bfloat16 or wider, within the bound.
No kernel may reach another device: no remote copies, remote signals or barrier semaphores. Data moves between devices by JAX's collectives and lax.ppermute only.
A program may use at most 64 MiB of HBM per device.

```python
import jax
import jax.numpy as jnp
from jax import lax

D = 4096
F = 1024
TOK_DEV = 384
CAP = 256
TOKENS = 24576
SLOTS = 16384
N_WIDE = 64
N_NARROW = 8


def draw_slot_count(key, part):
    key = jax.random.fold_in(key, 11)
    lowest = max(CAP // 4, 1)
    counts = jax.random.randint(key, (N_WIDE,), lowest, 3 * CAP // 4 + 1)
    fullest = jax.random.randint(jax.random.fold_in(key, 1), (), 0, N_WIDE)
    return counts.at[fullest].set(CAP).astype(jnp.int32)


def draw_slot_token(key, part):
    key = jax.random.fold_in(key, 12)
    device_keys = jax.random.split(key, N_WIDE)
    chosen = jax.vmap(lambda single: jax.random.permutation(single, TOK_DEV)[:CAP])(device_keys)
    return chosen.reshape(-1).astype(jnp.int32)


def levels(stream_key, dims, shards, least, high):
    def one(dim, blocks):
        heights = jax.random.uniform(jax.random.fold_in(jax.random.fold_in(stream_key, 6), dim), (blocks,), jnp.float32, least / len(shards), high / len(shards))
        return jnp.repeat(jnp.exp(heights), dims[dim] // blocks).reshape((-1,) + (1,) * (len(dims) - dim - 1))

    gain = one(*shards[0])
    for cut in shards[1:]:
        gain = gain * one(*cut)
    return gain


def centred(key, dims, deviation, bound, cuts=(), kind=jnp.bfloat16):
    array = jax.random.normal(key, dims, jnp.float32) * deviation
    if len(cuts) > 0:
        array = levels(key, dims, cuts, -0.22, 0.18) * array
    return jnp.clip(array, min=-bound, max=bound).astype(kind)


def setup_inputs(seed: int = 0) -> dict:
    keys = jax.random.split(jax.random.key(seed), 9)
    tokens = centred(keys[0], (TOKENS, D), 1.0, 6.0, ((0, 64), (1, 8)))
    grad_out = centred(keys[1], (TOKENS, D), 1.0, 6.0, ((0, 64), (1, 8)))
    slot_token = draw_slot_token(jax.random.fold_in(keys[8], 71), 0)
    slot_count = draw_slot_count(jax.random.fold_in(keys[8], 71), 0)
    slot_gate = jnp.clip(0.1 + 0.9 * jax.random.uniform(keys[4], (SLOTS,), jnp.float32) ** levels(keys[4], (SLOTS,), ((0, 64),), -0.2, 0.2), 0.1, 1.0)
    w_gate = centred(keys[5], (D, F), D ** -0.5, 0.09375, ((0, 64), (1, 8)))
    w_up = centred(keys[6], (D, F), D ** -0.5, 0.09375, ((0, 64), (1, 8)))
    w_down = centred(keys[7], (D, F), F ** -0.5, 0.1875, ((0, 64), (1, 8)))
    return dict(tokens=tokens, grad_out=grad_out, slot_token=slot_token, slot_count=slot_count, slot_gate=slot_gate, w_gate=w_gate, w_up=w_up, w_down=w_down)


def reference(tokens, grad_out, slot_token, slot_count, slot_gate, w_gate, w_up, w_down):
    f_block = F // N_NARROW
    owner = jnp.repeat(jnp.arange(N_WIDE, dtype=jnp.int32), CAP)
    row_index = (owner * TOK_DEV + slot_token).astype(jnp.int32)
    position = jnp.tile(jnp.arange(CAP, dtype=jnp.int32), N_WIDE)
    in_use = position < jnp.repeat(slot_count, CAP)
    weight_use = jnp.where(in_use, slot_gate, jnp.zeros_like(slot_gate))
    routed = tokens[row_index]
    pre_gate = jnp.dot(routed, w_gate, preferred_element_type=jnp.float32)
    pre_up = jnp.dot(routed, w_up, preferred_element_type=jnp.float32)
    sigma = jax.nn.sigmoid(pre_gate)
    hidden = (pre_gate * sigma * pre_up).astype(jnp.bfloat16)
    contract_last = (((1,), (1,)), ((), ()))
    contract_first = (((0,), (0,)), ((), ()))
    expert_out = jnp.zeros((routed.shape[0], D), jnp.float32)
    for which in range(N_NARROW):
        lower = which * f_block
        block = lax.dot_general(hidden[:, lower:lower + f_block], w_down[:, lower:lower + f_block],
                                contract_last, preferred_element_type=jnp.float32)
        expert_out = expert_out + lax.optimization_barrier(block.astype(jnp.bfloat16)).astype(jnp.float32)
    mixed = jnp.zeros((TOKENS, D), jnp.float32).at[row_index].add(weight_use[:, None] * expert_out)
    mixed = mixed.astype(jnp.bfloat16)
    grad_routed = (weight_use[:, None] * grad_out[row_index].astype(jnp.float32)).astype(jnp.bfloat16)
    grad_hidden = jnp.dot(grad_routed, w_down, preferred_element_type=jnp.float32)
    back_gate = (grad_hidden * pre_up * sigma * (1.0 + pre_gate * (1.0 - sigma))).astype(jnp.bfloat16)
    back_up = (grad_hidden * pre_gate * sigma).astype(jnp.bfloat16)
    grad_down = lax.dot_general(grad_routed, hidden, contract_first, preferred_element_type=jnp.float32)
    grad_gate = lax.dot_general(routed, back_gate, contract_first, preferred_element_type=jnp.float32)
    grad_up = lax.dot_general(routed, back_up, contract_first, preferred_element_type=jnp.float32)
    token_back = jnp.zeros((routed.shape[0], D), jnp.float32)
    for which in range(N_NARROW):
        lower = which * f_block
        block = lax.dot_general(back_gate[:, lower:lower + f_block], w_gate[:, lower:lower + f_block],
                                contract_last, preferred_element_type=jnp.float32)
        block = block + lax.dot_general(back_up[:, lower:lower + f_block], w_up[:, lower:lower + f_block],
                                        contract_last, preferred_element_type=jnp.float32)
        token_back = token_back + lax.optimization_barrier(block.astype(jnp.bfloat16)).astype(jnp.float32)
    grad_tokens = jnp.zeros((TOKENS, D), jnp.float32).at[row_index].add(token_back).astype(jnp.bfloat16)
    return mixed, grad_tokens, grad_gate, grad_up, grad_down
```

```python
import jax
import jax.numpy as jnp
from jax import lax
from jax.sharding import PartitionSpec as P

N_Y, N_Z, N_CORE, N_NARROW = 8, 4, 2, 8
F32, BF16 = jnp.float32, jnp.bfloat16


def wide_index(y, z, core):
    return (y * N_Z + z) * N_CORE + core


SWAP = [
    (
        wide_index(y, z, core) * N_NARROW + n,
        wide_index(core * 4 + n % 4, z, n // 4) * N_NARROW + y,
    )
    for y in range(N_Y)
    for z in range(N_Z)
    for core in range(N_CORE)
    for n in range(N_NARROW)
]
SWAP_BACK = [(b, a) for a, b in SWAP]
OTHER_CORE = [(w, w ^ 1) for w in range(N_Y * N_Z * N_CORE)]
CHIPS = [[wide_index(y, z, core) for y in range(N_Y) for z in range(N_Z)] for core in range(N_CORE)]


def dot(a, b, dims):
    return lax.dot_general(a, b, (dims, ((), ())), preferred_element_type=F32)


def spread(x, axis, groups=None):
    count = N_NARROW if groups is None else len(groups[0])
    return lax.all_to_all(
        jnp.broadcast_to(x[None], (count,) + x.shape), axis, 0, 0, axis_index_groups=groups
    )


def local(tokens, grad_out, slot_token, slot_count, slot_gate, w_gate, w_up, w_down):
    slots, tok = slot_token.shape[0], tokens.shape[0]
    feat = tokens.shape[1]
    rows, cols = w_gate.shape
    block = lax.ppermute(jnp.concatenate((w_gate, w_up, w_down), axis=0), ("wide", "narrow"), SWAP)
    pieces = spread(block, "wide", CHIPS).reshape(2, 4, N_Z, 3, rows, cols)
    weights = pieces.transpose(3, 2, 0, 4, 1, 5).reshape(3, feat, 4 * cols)
    wg, wu, wd = weights[0], weights[1], weights[2]

    weight_use = jnp.where(lax.iota(jnp.int32, slots) < slot_count[0], slot_gate, 0.0)
    pick = (slot_token[:, None] == lax.broadcasted_iota(jnp.int32, (slots, tok), 1)).astype(BF16)
    own_x = dot(pick, tokens, ((1,), (0,))).astype(BF16)
    own_g = (weight_use[:, None] * dot(pick, grad_out, ((1,), (0,)))).astype(BF16)
    other = lax.ppermute(jnp.stack((own_x, own_g)), "wide", OTHER_CORE)
    x = jnp.concatenate((own_x, other[0]), axis=0)
    g = jnp.concatenate((own_g, other[1]), axis=0)

    part = jnp.concatenate(
        (dot(x, wg, ((1,), (0,))), dot(x, wu, ((1,), (0,))), dot(g, wd, ((1,), (0,)))), axis=1
    ).astype(BF16)
    units = wg.shape[1]
    got = lax.all_to_all(part.reshape(N_NARROW, -1, 3 * units), "narrow", 0, 0)
    full = got.astype(F32).sum(axis=0)
    pre_gate, pre_up, grad_hidden = full[:, :units], full[:, units : 2 * units], full[:, 2 * units :]
    sigma = jax.nn.sigmoid(pre_gate)
    acts = jnp.concatenate(
        (
            grad_hidden * pre_up * sigma * (1.0 + pre_gate * (1.0 - sigma)),
            grad_hidden * pre_gate * sigma,
            pre_gate * sigma * pre_up,
        ),
        axis=1,
    ).astype(BF16)
    acts = spread(acts, "narrow").reshape(2 * slots, 3 * units)
    back_gate, back_up, hidden = acts[:, :units], acts[:, units : 2 * units], acts[:, 2 * units :]

    terms = jnp.stack(
        (
            dot(x, back_gate, ((0,), (0,))),
            dot(x, back_up, ((0,), (0,))),
            dot(g, hidden, ((0,), (0,))),
        )
    ).astype(BF16)
    terms = terms.reshape(3, N_Z, 2, rows, 4, cols).transpose(2, 4, 1, 0, 3, 5)
    terms = lax.all_to_all(terms.reshape(-1, 3 * rows, cols), "wide", 0, 0, axis_index_groups=CHIPS)
    grads = terms.astype(F32).sum(axis=0).astype(BF16)
    grads = lax.ppermute(grads, ("wide", "narrow"), SWAP_BACK).astype(F32)

    out = dot(hidden, wd, ((1,), (1,)))
    back = dot(back_gate, wg, ((1,), (1,))) + dot(back_up, wu, ((1,), (1,)))
    theirs = lax.ppermute(
        jnp.stack((out[slots:], back[slots:])).astype(BF16), "wide", OTHER_CORE
    ).astype(F32)
    out = (weight_use[:, None] * (out[:slots] + theirs[0])).astype(BF16)
    back = (back[:slots] + theirs[1]).astype(BF16)
    mixed = dot(pick, out, ((0,), (0,))).astype(BF16)
    grad_tokens = dot(pick, back, ((0,), (0,))).astype(BF16)
    return mixed, grad_tokens, grads[:rows], grads[rows : 2 * rows], grads[2 * rows :]


def solution(mesh):
    both = P("wide", "narrow")
    in_specs = (both, both, P("wide"), P("wide"), P("wide"), both, both, both)
    return jax.shard_map(
        local, mesh=mesh, in_specs=in_specs, out_specs=(both,) * 5, check_vma=False
    )
```

```python
import jax
import jax.numpy as jnp
from jax import lax
from jax.sharding import PartitionSpec as P

N_Y, N_Z, N_CORE, N_X = 8, 4, 2, 4
N_WIDE, N_NARROW = N_Y * N_Z * N_CORE, 2 * N_X
F32, BF16 = jnp.float32, jnp.bfloat16


def wide_index(y, z, core):
    return (y * N_Z + z) * N_CORE + core


def swap_pairs():
    pairs = []
    for y in range(N_Y):
        for z in range(N_Z):
            for core in range(N_CORE):
                for n in range(N_NARROW):
                    z_bit, to_core, half = n // 4, n // 2 % 2, n % 2
                    to = wide_index(half * 4 + z % 2 * 2 + core, z // 2 * 2 + z_bit, to_core)
                    pairs.append((wide_index(y, z, core) * N_NARROW + n, to * N_NARROW + y))
    return pairs


SWAP = swap_pairs()
SWAP_BACK = [(b, a) for a, b in SWAP]
OTHER_CORE = [(w, w ^ 1) for w in range(N_WIDE)]
OTHER_CHIP = [(w, w ^ 2) for w in range(N_WIDE)]
OTHER_HALF = [(n, n ^ 1) for n in range(N_NARROW)]
OWNERS = [
    [wide_index(y, 2 * pair + z_bit, core) for y in range(N_Y) for pair in range(2)]
    for z_bit in range(2)
    for core in range(N_CORE)
]
ALONG_X = [[2 * x + z_hi for x in range(N_X)] for z_hi in range(2)]


def dot(a, b, dims):
    return lax.dot_general(a, b, (dims, ((), ())), preferred_element_type=F32)


def exchange(x, axis, groups):
    return lax.all_to_all(x, axis, 0, 0, axis_index_groups=groups)


def spread(x, axis, groups):
    return exchange(jnp.broadcast_to(x[None], (len(groups[0]),) + x.shape), axis, groups)


def local(tokens, grad_out, slot_token, slot_count, slot_gate, w_gate, w_up, w_down):
    slots, tok = slot_token.shape[0], tokens.shape[0]
    feat = tokens.shape[1]
    rows, cols = w_gate.shape
    half = slots // 2
    z_hi = lax.axis_index("narrow") % 2

    def mine_first(a):
        return jnp.where(z_hi == 0, a, jnp.concatenate((a[half:], a[:half])))

    block = lax.ppermute(jnp.concatenate((w_gate, w_up, w_down), axis=0), ("wide", "narrow"), SWAP)
    pieces = spread(block, "wide", OWNERS).reshape(2, 2, 2, 2, 3, rows, cols)
    weights = pieces.transpose(4, 3, 1, 2, 5, 0, 6).reshape(3, feat, 2 * cols)
    wg, wu, wd = weights[0], weights[1], weights[2]

    weight_use = jnp.where(lax.iota(jnp.int32, slots) < slot_count[0], slot_gate, 0.0)
    weight_use, slot_token = mine_first(weight_use), mine_first(slot_token)
    pick = (slot_token[:, None] == lax.broadcasted_iota(jnp.int32, (slots, tok), 1)).astype(BF16)
    own_x = dot(pick, tokens, ((1,), (0,))).astype(BF16)
    own_g = (weight_use[:, None] * dot(pick, grad_out, ((1,), (0,)))).astype(BF16)
    own = jnp.stack((own_x, own_g))
    chip = jnp.concatenate((own, lax.ppermute(own, "wide", OTHER_CHIP)), axis=1)
    all_rows = jnp.concatenate((chip, lax.ppermute(chip, "wide", OTHER_CORE)), axis=1)
    x, g = all_rows[0], all_rows[1]

    part = jnp.concatenate(
        (dot(x, wg, ((1,), (0,))), dot(x, wu, ((1,), (0,))), dot(g, wd, ((1,), (0,)))), axis=1
    ).astype(BF16)
    units = wg.shape[1]
    got = exchange(part.reshape(N_X, slots, 3 * units), "narrow", ALONG_X)
    part = got.astype(F32).sum(axis=0)
    theirs = lax.ppermute(part[half:].astype(BF16), "narrow", OTHER_HALF)
    full = part[:half] + theirs.astype(F32)
    pre_gate, pre_up, grad_hidden = full[:, :units], full[:, units : 2 * units], full[:, 2 * units :]
    sigma = jax.nn.sigmoid(pre_gate)
    acts = jnp.concatenate(
        (
            grad_hidden * pre_up * sigma * (1.0 + pre_gate * (1.0 - sigma)),
            grad_hidden * pre_gate * sigma,
            pre_gate * sigma * pre_up,
        ),
        axis=1,
    ).astype(BF16)
    acts = jnp.concatenate((acts, lax.ppermute(acts, "narrow", OTHER_HALF)))
    acts = spread(acts, "narrow", ALONG_X).reshape(N_X * slots, 3 * units)
    back_gate, back_up, hidden = acts[:, :units], acts[:, units : 2 * units], acts[:, 2 * units :]

    terms = jnp.stack(
        (
            dot(x, back_gate, ((0,), (0,))),
            dot(x, back_up, ((0,), (0,))),
            dot(g, hidden, ((0,), (0,))),
        )
    ).astype(BF16)
    terms = terms.reshape(3, 2, 2, 2, rows, 2, cols).transpose(5, 2, 3, 1, 0, 4, 6)
    terms = exchange(terms.reshape(-1, 3 * rows, cols), "wide", OWNERS)
    grads = terms.astype(F32).sum(axis=0).astype(BF16)
    grads = lax.ppermute(grads, ("wide", "narrow"), SWAP_BACK).astype(F32)

    outs = jnp.stack(
        (
            dot(hidden, wd, ((1,), (1,))),
            dot(back_gate, wg, ((1,), (1,))) + dot(back_up, wu, ((1,), (1,))),
        )
    )
    theirs = lax.ppermute(outs[:, 2 * slots :].astype(BF16), "wide", OTHER_CORE)
    outs = outs[:, : 2 * slots] + theirs.astype(F32)
    theirs = lax.ppermute(outs[:, slots:].astype(BF16), "wide", OTHER_CHIP)
    outs = outs[:, :slots] + theirs.astype(F32)
    out = (weight_use[:, None] * outs[0]).astype(BF16)
    mixed = dot(pick, out, ((0,), (0,))).astype(BF16)
    grad_tokens = dot(pick, outs[1].astype(BF16), ((0,), (0,))).astype(BF16)
    return mixed, grad_tokens, grads[:rows], grads[rows : 2 * rows], grads[2 * rows :]


def solution(mesh):
    both = P("wide", "narrow")
    in_specs = (both, both, P("wide"), P("wide"), P("wide"), both, both, both)
    return jax.shard_map(
        local, mesh=mesh, in_specs=in_specs, out_specs=(both,) * 5, check_vma=False
    )
```

```python
import jax
import jax.numpy as jnp
from jax import lax
from jax.experimental import pallas as pl
from jax.experimental.pallas import tpu as pltpu
from jax.sharding import PartitionSpec as P

N_Y, N_Z, N_CORE, N_X = 8, 4, 2, 4
N_WIDE, N_NARROW = N_Y * N_Z * N_CORE, 2 * N_X
F32, BF16 = jnp.float32, jnp.bfloat16
FIRST, LAST, PLAIN = ((0,), (0,)), ((1,), (1,)), ((1,), (0,))


def wide_index(y, z, core):
    return (y * N_Z + z) * N_CORE + core


def swap_pairs():
    pairs = []
    for y in range(N_Y):
        for z in range(N_Z):
            for core in range(N_CORE):
                for n in range(N_NARROW):
                    z_bit, to_core, half = n // 4, n // 2 % 2, n % 2
                    to = wide_index(half * 4 + z % 2 * 2 + core, z // 2 * 2 + z_bit, to_core)
                    pairs.append((wide_index(y, z, core) * N_NARROW + n, to * N_NARROW + y))
    return pairs


PIECES = [(i // 8, (i % 2 * 2 + i // 4 % 2) * 2 + i // 2 % 2) for i in range(16)]
SWAP = swap_pairs()
SWAP_BACK = [(b, a) for a, b in SWAP]
OTHER_CORE = [(w, w ^ 1) for w in range(N_WIDE)]
OTHER_CHIP = [(w, w ^ 2) for w in range(N_WIDE)]
OTHER_HALF = [(n, n ^ 1) for n in range(N_NARROW)]
OWNERS = [
    [wide_index(y, 2 * pair + z_bit, core) for y in range(N_Y) for pair in range(2)]
    for z_bit in range(2)
    for core in range(N_CORE)
]
ALONG_X = [[2 * x + z_hi for x in range(N_X)] for z_hi in range(2)]


def dot(a, b, dims=PLAIN):
    return lax.dot_general(a, b, (dims, ((), ())), preferred_element_type=F32)


def exchange(x, axis, groups):
    return lax.all_to_all(x, axis, 0, 0, axis_index_groups=groups)


def call(body, outs, flops, *args):
    size = sum(a.size * a.dtype.itemsize for a in args)
    spec = pl.BlockSpec(memory_space=pltpu.VMEM)
    return pl.pallas_call(
        body,
        out_shape=[jax.ShapeDtypeStruct(shape, kind) for shape, kind in outs],
        in_specs=[spec] * len(args),
        out_specs=[spec] * len(outs),
        compiler_params=pltpu.CompilerParams(vmem_limit_bytes=32 * 1024 * 1024),
        cost_estimate=pl.CostEstimate(flops=flops, bytes_accessed=size, transcendentals=0),
    )(*args)


def use_of(gate, count):
    slots = gate.shape[1]
    lane = lax.broadcasted_iota(jnp.int32, (1, slots), 1)
    use = jnp.where(lane < count, gate, 0.0)
    square = lax.broadcasted_iota(jnp.int32, (slots, slots), 0) == lax.broadcasted_iota(
        jnp.int32, (slots, slots), 1
    )
    return jnp.sum(jnp.where(square, use, 0.0), axis=1, keepdims=True)


def pick_of(token, tok):
    slots = token.shape[1]
    return jnp.where(lax.broadcasted_iota(jnp.int32, (tok, slots), 0) == token, 1.0, 0.0).astype(BF16)


def rows_body(tokens, grad_out, token, count, gate, w_gate, w_up, w_down, own, block):
    rows = w_gate.shape[0]
    block[0:rows] = w_gate[...]
    block[rows : 2 * rows] = w_up[...]
    block[2 * rows : 3 * rows] = w_down[...]
    pick = pick_of(token[...], tokens.shape[0])
    own[0] = dot(pick, tokens[...], FIRST).astype(BF16)
    own[1] = (use_of(gate[...], count[...]) * dot(pick, grad_out[...], FIRST)).astype(BF16)


def forward_body(pieces, a0, a1, b0, b1, part_b, part_a, weights):
    rows = pieces.shape[1] // 3
    cols = pieces.shape[2]
    for i, (half, place) in enumerate(PIECES):
        for m in range(3):
            weights[m, rows * place : rows * (place + 1), cols * half : cols * (half + 1)] = pieces[
                i, rows * m : rows * (m + 1)
            ]
    units = 2 * cols
    slots = a0.shape[1]
    for part, x0, x1 in ((part_b, b0, b1), (part_a, a0, a1)):
        for which, x in enumerate((x0, x1)):
            at = slice(slots * which, slots * (which + 1))
            for m in range(3):
                part[at, units * m : units * (m + 1)] = dot(x[m // 2], weights[m]).astype(BF16)


def act_body(got, theirs, acts):
    total = got[0].astype(F32)
    for i in range(1, got.shape[0]):
        total = total + got[i].astype(F32)
    total = total + theirs[...].astype(F32)
    units = total.shape[1] // 3
    pre_gate, pre_up, grad_hidden = total[:, :units], total[:, units : 2 * units], total[:, 2 * units :]
    sigma = jax.nn.sigmoid(pre_gate)
    back_gate = (grad_hidden * pre_up * sigma * (1.0 + pre_gate * (1.0 - sigma))).astype(BF16)
    back_up = (grad_hidden * pre_gate * sigma).astype(BF16)
    hidden = (pre_gate * sigma * pre_up).astype(BF16)
    for i in range(got.shape[0]):
        acts[i, :, :units] = back_gate
        acts[i, :, units : 2 * units] = back_up
        acts[i, :, 2 * units :] = hidden


def outputs(acts, weights, which):
    units = weights.shape[2]
    if which == 0:
        return dot(acts[:, 2 * units :], weights[2], LAST)
    return dot(acts[:, :units], weights[0], LAST) + dot(acts[:, units : 2 * units], weights[1], LAST)


def term(acts, x0, x1, m, units):
    slots = x0.shape[1]
    cut = slice(units * m, units * (m + 1))
    return dot(x0[m // 2], acts[:slots, cut], FIRST) + dot(x1[m // 2], acts[slots:, cut], FIRST)


def theirs_body(acts, x0, x1, weights, send, terms):
    units = weights.shape[2]
    for which in range(2):
        send[which] = outputs(acts, weights, which).astype(BF16)
    for m in range(3):
        terms[:, units * m : units * (m + 1)] = term(acts, x0, x1, m, units)


def ours_body(acts, x0, x1, weights, terms, got, pieces, mine, send):
    units = weights.shape[2]
    rows, cols = pieces.shape[1] // 3, pieces.shape[2]
    slots = x0.shape[1]
    for m in range(3):
        total = (terms[:, units * m : units * (m + 1)] + term(acts, x0, x1, m, units)).astype(BF16)
        for i, (half, place) in enumerate(PIECES):
            pieces[i, rows * m : rows * (m + 1)] = total[
                rows * place : rows * (place + 1), cols * half : cols * (half + 1)
            ]
    for which in range(2):
        out = outputs(acts, weights, which) + got[which].astype(F32)
        mine[which] = out[:slots]
        send[which] = out[slots:].astype(BF16)


def tokens_body(mine, got, token, count, gate, mixed, grad_tokens):
    pick = pick_of(token[...], mixed.shape[0])
    out = use_of(gate[...], count[...]) * (mine[0] + got[0].astype(F32))
    mixed[...] = dot(pick, out.astype(BF16)).astype(BF16)
    back = mine[1] + got[1].astype(F32)
    grad_tokens[...] = dot(pick, back.astype(BF16)).astype(BF16)


def local(tokens, grad_out, slot_token, slot_count, slot_gate, w_gate, w_up, w_down):
    slots, (tok, feat) = slot_token.shape[0], tokens.shape
    rows, cols = w_gate.shape
    units = 2 * cols
    token, gate, count = slot_token[None], slot_gate[None], slot_count[None]
    pick_flops = 4 * slots * tok * feat
    own, block = call(
        rows_body,
        [((2, slots, feat), BF16), ((3 * rows, cols), BF16)],
        pick_flops,
        *(tokens, grad_out, token, count, gate, w_gate, w_up, w_down),
    )

    block = lax.ppermute(block, ("wide", "narrow"), SWAP)
    next_own = lax.ppermute(own, "wide", OTHER_CHIP)
    core_own = lax.ppermute(own, "wide", OTHER_CORE)
    core_next = lax.ppermute(next_own, "wide", OTHER_CORE)
    pieces = exchange(jnp.broadcast_to(block[None], (len(PIECES),) + block.shape), "wide", OWNERS)

    flops = 2 * 3 * 2 * slots * feat * units
    part_b, part_a, weights = call(
        forward_body,
        [((2 * slots, 3 * units), BF16)] * 2 + [((3, feat, units), BF16)],
        2 * flops,
        *(pieces, own, next_own, core_own, core_next),
    )
    portion = 2 * slots // N_X
    parts = (N_X, portion, 3 * units)

    def narrow_sum(part):
        got = exchange(part.reshape(parts), "narrow", ALONG_X)
        sent = got.astype(F32).sum(axis=0).astype(BF16)
        return got, lax.ppermute(sent, "narrow", OTHER_HALF)

    def activations(got, theirs):
        (acts,) = call(act_body, [(parts, BF16)], 20 * portion * 3 * units, got, theirs)
        return exchange(acts, "narrow", ALONG_X).reshape(2 * slots, 3 * units)

    got_b, theirs_b = narrow_sum(part_b)
    part_a, got_b = lax.optimization_barrier((part_a, got_b))
    got_a, theirs_a = narrow_sum(part_a)
    acts_b = activations(got_b, theirs_b)
    acts_a = activations(got_a, theirs_a)

    send, terms = call(
        theirs_body,
        [((2, 2 * slots, feat), BF16), ((feat, 3 * units), F32)],
        2 * flops,
        *(acts_b, core_own, core_next, weights),
    )
    got = lax.ppermute(send, "wide", OTHER_CORE)
    terms, mine, send = call(
        ours_body,
        [(pieces.shape, BF16), ((2, slots, feat), F32), ((2, slots, feat), BF16)],
        2 * flops,
        *(acts_a, own, next_own, weights, terms, got),
    )
    got = lax.ppermute(send, "wide", OTHER_CHIP)
    terms = exchange(terms, "wide", OWNERS)
    mixed, grad_tokens = call(
        tokens_body, [((tok, feat), BF16)] * 2, pick_flops, *(mine, got, token, count, gate)
    )
    terms, mixed, grad_tokens = lax.optimization_barrier((terms, mixed, grad_tokens))
    grads = terms.astype(F32).sum(axis=0).astype(BF16)
    grads = lax.ppermute(grads, ("wide", "narrow"), SWAP_BACK).astype(F32)
    return mixed, grad_tokens, grads[:rows], grads[rows : 2 * rows], grads[2 * rows :]


def solution(mesh):
    both = P("wide", "narrow")
    in_specs = (both, both, P("wide"), P("wide"), P("wide"), both, both, both)
    return jax.shard_map(
        local, mesh=mesh, in_specs=in_specs, out_specs=(both,) * 5, check_vma=False
    )
```

```python
import jax
import jax.numpy as jnp
from jax import lax
from jax.experimental import pallas as pl
from jax.experimental.pallas import tpu as pltpu
from jax.sharding import PartitionSpec as P

N_Y, N_Z, N_CORE, N_X = 8, 4, 2, 4
N_WIDE, N_NARROW = N_Y * N_Z * N_CORE, 2 * N_X
F32, BF16 = jnp.float32, jnp.bfloat16
FIRST, LAST, PLAIN = ((0,), (0,)), ((1,), (1,)), ((1,), (0,))


def wide_index(y, z, core):
    return (y * N_Z + z) * N_CORE + core


def swap_pairs():
    pairs = []
    for y in range(N_Y):
        for z in range(N_Z):
            for core in range(N_CORE):
                for n in range(N_NARROW):
                    z_bit, to_core, half = n // 4, n // 2 % 2, n % 2
                    to = wide_index(half * 4 + z % 2 * 2 + core, z // 2 * 2 + z_bit, to_core)
                    pairs.append((wide_index(y, z, core) * N_NARROW + n, to * N_NARROW + y))
    return pairs


PIECES = [(i // 8, (i % 2 * 2 + i // 4 % 2) * 2 + i // 2 % 2) for i in range(16)]
SWAP = swap_pairs()
SWAP_BACK = [(b, a) for a, b in SWAP]
OTHER_CORE = [(w, w ^ 1) for w in range(N_WIDE)]
OTHER_CHIP = [(w, w ^ 2) for w in range(N_WIDE)]
OTHER_HALF = [(n, n ^ 1) for n in range(N_NARROW)]
OWNERS = [
    [wide_index(y, 2 * pair + z_bit, core) for y in range(N_Y) for pair in range(2)]
    for z_bit in range(2)
    for core in range(N_CORE)
]
ALONG_X = [[2 * x + z_hi for x in range(N_X)] for z_hi in range(2)]


def dot(a, b, dims=PLAIN):
    return lax.dot_general(a, b, (dims, ((), ())), preferred_element_type=F32)


def exchange(x, axis, groups):
    return lax.all_to_all(x, axis, 0, 0, axis_index_groups=groups)


def call(body, outs, flops, *args, after=(), fetch=False):
    size = sum(a.size * a.dtype.itemsize for a in args)
    vmem, anywhere = pl.BlockSpec(memory_space=pltpu.VMEM), pl.BlockSpec(memory_space=pl.ANY)
    scratch = ()
    if fetch:
        scratch = [pltpu.VMEM(a.shape, a.dtype) for a in args] + [pltpu.SemaphoreType.DMA((len(args),))]

    def inner(*refs):
        body(*refs[: len(args)], *refs[len(args) + len(after) :])

    return pl.pallas_call(
        inner,
        out_shape=[jax.ShapeDtypeStruct(shape, kind) for shape, kind in outs],
        in_specs=[pl.BlockSpec(memory_space=pltpu.HBM) if fetch else vmem] * len(args) + [anywhere] * len(after),
        out_specs=[vmem] * len(outs),
        scratch_shapes=scratch,
        compiler_params=pltpu.CompilerParams(vmem_limit_bytes=(60 if fetch else 12) * 1024 * 1024),
        cost_estimate=pl.CostEstimate(flops=flops, bytes_accessed=size, transcendentals=0),
    )(*args, *after)


def use_of(gate, count):
    slots = gate.shape[1]
    lane = lax.broadcasted_iota(jnp.int32, (1, slots), 1)
    use = jnp.where(lane < count, gate, 0.0)
    square = lax.broadcasted_iota(jnp.int32, (slots, slots), 0) == lax.broadcasted_iota(
        jnp.int32, (slots, slots), 1
    )
    return jnp.sum(jnp.where(square, use, 0.0), axis=1, keepdims=True)


def pick_of(token, tok):
    slots = token.shape[1]
    return jnp.where(lax.broadcasted_iota(jnp.int32, (tok, slots), 0) == token, 1.0, 0.0).astype(BF16)


def rows_body(*refs):
    sources, (own, block), held, sem = refs[:8], refs[8:10], refs[10:18], refs[18]
    copies = [pltpu.make_async_copy(s, h, sem.at[i]) for i, (s, h) in enumerate(zip(sources, held))]
    for copy in copies:
        copy.start()
    tokens, grad_out, token, count, gate, w_gate, w_up, w_down = held
    rows = w_gate.shape[0]
    for i, weight in ((5, w_gate), (6, w_up), (7, w_down)):
        copies[i].wait()
        block[rows * (i - 5) : rows * (i - 4)] = weight[...]
    for i in (2, 3, 4, 0):
        copies[i].wait()
    pick = pick_of(token[...], tokens.shape[0])
    own[0] = dot(pick, tokens[...], FIRST).astype(BF16)
    copies[1].wait()
    own[1] = (use_of(gate[...], count[...]) * dot(pick, grad_out[...], FIRST)).astype(BF16)


def products(part, x0, x1, weights):
    slots, units = x0.shape[1], weights.shape[2]
    for which, x in enumerate((x0, x1)):
        for m in range(3):
            part[slots * which : slots * (which + 1), units * m : units * (m + 1)] = dot(
                x[m // 2], weights[m]
            ).astype(BF16)


def first_body(pieces, x0, x1, part, weights):
    rows, cols = pieces.shape[1] // 3, pieces.shape[2]
    for i, (half, place) in enumerate(PIECES):
        for m in range(3):
            weights[m, rows * place : rows * (place + 1), cols * half : cols * (half + 1)] = pieces[
                i, rows * m : rows * (m + 1)
            ]
    products(part, x0, x1, weights)


def second_body(weights, x0, x1, part):
    products(part, x0, x1, weights)


def act_body(got, theirs, acts):
    total = got[0].astype(F32)
    for i in range(1, got.shape[0]):
        total = total + got[i].astype(F32)
    total = total + theirs[...].astype(F32)
    units = total.shape[1] // 3
    pre_gate, pre_up, grad_hidden = total[:, :units], total[:, units : 2 * units], total[:, 2 * units :]
    sigma = jax.nn.sigmoid(pre_gate)
    back_gate = (grad_hidden * pre_up * sigma * (1.0 + pre_gate * (1.0 - sigma))).astype(BF16)
    back_up = (grad_hidden * pre_gate * sigma).astype(BF16)
    hidden = (pre_gate * sigma * pre_up).astype(BF16)
    for i in range(got.shape[0]):
        acts[i, :, :units] = back_gate
        acts[i, :, units : 2 * units] = back_up
        acts[i, :, 2 * units :] = hidden


def outputs(acts, weights, which):
    units = weights.shape[2]
    if which == 0:
        return dot(acts[:, 2 * units :], weights[2], LAST)
    return dot(acts[:, :units], weights[0], LAST) + dot(acts[:, units : 2 * units], weights[1], LAST)


def term(acts, x0, x1, m, units):
    slots = x0.shape[1]
    cut = slice(units * m, units * (m + 1))
    return dot(x0[m // 2], acts[:slots, cut], FIRST) + dot(x1[m // 2], acts[slots:, cut], FIRST)


def near_body(acts, x0, x1, weights, mine, send, terms):
    units, slots = weights.shape[2], x0.shape[1]
    for which in range(2):
        out = outputs(acts, weights, which)
        mine[which] = out[:slots]
        send[which] = out[slots:].astype(BF16)
    for m in range(3):
        terms[:, units * m : units * (m + 1)] = term(acts, x0, x1, m, units)


def far_body(acts, weights, mine, send):
    slots = mine.shape[1]
    for which in range(2):
        out = outputs(acts, weights, which)
        mine[which] = out[:slots]
        send[which] = out[slots:].astype(BF16)


def terms_body(acts, x0, x1, terms, pieces):
    units = terms.shape[1] // 3
    rows, cols = pieces.shape[1] // 3, pieces.shape[2]
    for m in range(3):
        total = (terms[:, units * m : units * (m + 1)] + term(acts, x0, x1, m, units)).astype(BF16)
        for i, (half, place) in enumerate(PIECES):
            pieces[i, rows * m : rows * (m + 1)] = total[
                rows * place : rows * (place + 1), cols * half : cols * (half + 1)
            ]


def tokens_body(mine, core, chip, token, count, gate, mixed, grad_tokens):
    pick = pick_of(token[...], mixed.shape[0])
    out, back = [mine[i] + core[i].astype(F32) + chip[i].astype(F32) for i in range(2)]
    mixed[...] = dot(pick, (use_of(gate[...], count[...]) * out).astype(BF16)).astype(BF16)
    grad_tokens[...] = dot(pick, back.astype(BF16)).astype(BF16)


def local(tokens, grad_out, slot_token, slot_count, slot_gate, w_gate, w_up, w_down):
    slots, (tok, feat) = slot_token.shape[0], tokens.shape
    rows, cols = w_gate.shape
    units = 2 * cols
    token, gate, count = slot_token[None], slot_gate[None], slot_count[None]
    pick_flops = 4 * slots * tok * feat
    own, block = call(
        rows_body,
        [((2, slots, feat), BF16), ((3 * rows, cols), BF16)],
        pick_flops,
        *(tokens, grad_out, token, count, gate, w_gate, w_up, w_down),
        fetch=True,
    )

    block = lax.ppermute(block, ("wide", "narrow"), SWAP)
    chip_own = lax.ppermute(own, "wide", OTHER_CHIP)
    core_own = lax.ppermute(own, "wide", OTHER_CORE)
    core_chip = lax.ppermute(chip_own, "wide", OTHER_CORE)
    pieces = exchange(jnp.broadcast_to(block[None], (len(PIECES),) + block.shape), "wide", OWNERS)

    flops = 2 * 3 * 2 * slots * feat * units
    wide_part = ((2 * slots, 3 * units), BF16)
    part_1, weights = call(
        first_body, [wide_part, ((3, feat, units), BF16)], flops, pieces, own, core_own
    )
    (part_2,) = call(second_body, [wide_part], flops, weights, chip_own, core_chip)
    portion = 2 * slots // N_X
    parts = (N_X, portion, 3 * units)

    def narrow_sum(part):
        got = exchange(part.reshape(parts), "narrow", ALONG_X)
        sent = got.astype(F32).sum(axis=0).astype(BF16)
        return got, lax.ppermute(sent, "narrow", OTHER_HALF)

    def activations(got, theirs, after):
        (acts,) = call(
            act_body, [(parts, BF16)], 20 * portion * 3 * units, got, theirs, after=after
        )
        return exchange(acts, "narrow", ALONG_X).reshape(2 * slots, 3 * units)

    got_1, theirs_1 = narrow_sum(part_1)
    got_2, theirs_2 = narrow_sum(part_2)
    acts_1 = activations(got_1, theirs_1, (got_2,))
    acts_2 = activations(got_2, theirs_2, (acts_1,))

    mine, send, terms = call(
        near_body,
        [((2, slots, feat), F32), ((2, slots, feat), BF16), ((feat, 3 * units), F32)],
        2 * flops,
        *(acts_1, own, core_own, weights),
    )
    core = lax.ppermute(send, "wide", OTHER_CORE)
    far, send = call(
        far_body, [((2, slots, feat), F32), ((2, slots, feat), BF16)], flops, acts_2, weights
    )
    far = (far + lax.ppermute(send, "wide", OTHER_CORE).astype(F32)).astype(BF16)
    (terms,) = call(
        terms_body, [(pieces.shape, BF16)], flops, acts_2, chip_own, core_chip, terms
    )
    chip = lax.ppermute(far, "wide", OTHER_CHIP)
    terms = exchange(terms, "wide", OWNERS)
    grads = terms.astype(F32).sum(axis=0).astype(BF16)
    grads = lax.ppermute(grads, ("wide", "narrow"), SWAP_BACK).astype(F32)
    mixed, grad_tokens = call(
        tokens_body, [((tok, feat), BF16)] * 2, pick_flops, *(mine, core, chip, token, count, gate)
    )
    return mixed, grad_tokens, grads[:rows], grads[rows : 2 * rows], grads[2 * rows :]


def solution(mesh):
    both = P("wide", "narrow")
    in_specs = (both, both, P("wide"), P("wide"), P("wide"), both, both, both)
    return jax.shard_map(
        local, mesh=mesh, in_specs=in_specs, out_specs=(both,) * 5, check_vma=False
    )
```

```python
import jax
import jax.numpy as jnp
from jax import lax
from jax.experimental import pallas as pl
from jax.experimental.pallas import tpu as pltpu
from jax.sharding import PartitionSpec as P

N_Y, N_Z, N_CORE, N_X = 8, 4, 2, 4
N_WIDE, N_NARROW = N_Y * N_Z * N_CORE, 2 * N_X
F32, BF16 = jnp.float32, jnp.bfloat16
FIRST, LAST, PLAIN = ((0,), (0,)), ((1,), (1,)), ((1,), (0,))


def wide_index(y, z, core):
    return (y * N_Z + z) * N_CORE + core


def swap_pairs():
    pairs = []
    for y in range(N_Y):
        for z in range(N_Z):
            for core in range(N_CORE):
                for n in range(N_NARROW):
                    z_bit, to_core, half = n // 4, n // 2 % 2, n % 2
                    to = wide_index(half * 4 + z % 2 * 2 + core, z // 2 * 2 + z_bit, to_core)
                    pairs.append((wide_index(y, z, core) * N_NARROW + n, to * N_NARROW + y))
    return pairs


PIECES = [(i // 8, (i % 2 * 2 + i // 4 % 2) * 2 + i // 2 % 2) for i in range(16)]
SWAP = swap_pairs()
SWAP_BACK = [(b, a) for a, b in SWAP]
OTHER_CORE = [(w, w ^ 1) for w in range(N_WIDE)]
OTHER_CHIP = [(w, w ^ 2) for w in range(N_WIDE)]
OTHER_HALF = [(n, n ^ 1) for n in range(N_NARROW)]
OWNERS = [
    [wide_index(y, 2 * pair + z_bit, core) for y in range(N_Y) for pair in range(2)]
    for z_bit in range(2)
    for core in range(N_CORE)
]
ALONG_X = [[2 * x + z_hi for x in range(N_X)] for z_hi in range(2)]


def dot(a, b, dims=PLAIN):
    return lax.dot_general(a, b, (dims, ((), ())), preferred_element_type=F32)


def exchange(x, axis, groups):
    return lax.all_to_all(x, axis, 0, 0, axis_index_groups=groups)


def call(body, outs, flops, *args, after=(), fetch=False, grant=12):
    size = sum(a.size * a.dtype.itemsize for a in args)
    vmem, anywhere = pl.BlockSpec(memory_space=pltpu.VMEM), pl.BlockSpec(memory_space=pl.ANY)
    scratch = ()
    if fetch:
        scratch = [pltpu.VMEM(a.shape, a.dtype) for a in args] + [pltpu.SemaphoreType.DMA((len(args),))]

    def inner(*refs):
        body(*refs[: len(args)], *refs[len(args) + len(after) :])

    return pl.pallas_call(
        inner,
        out_shape=[jax.ShapeDtypeStruct(shape, kind) for shape, kind in outs],
        in_specs=[pl.BlockSpec(memory_space=pltpu.HBM) if fetch else vmem] * len(args) + [anywhere] * len(after),
        out_specs=[vmem] * len(outs),
        scratch_shapes=scratch,
        compiler_params=pltpu.CompilerParams(vmem_limit_bytes=grant * 1024 * 1024),
        cost_estimate=pl.CostEstimate(flops=flops, bytes_accessed=size, transcendentals=0),
    )(*args, *after)


def use_of(gate, count):
    slots = gate.shape[1]
    lane = lax.broadcasted_iota(jnp.int32, (1, slots), 1)
    use = jnp.where(lane < count, gate, 0.0)
    square = lax.broadcasted_iota(jnp.int32, (slots, slots), 0) == lax.broadcasted_iota(
        jnp.int32, (slots, slots), 1
    )
    return jnp.sum(jnp.where(square, use, 0.0), axis=1, keepdims=True)


def pick_of(token, tok):
    slots = token.shape[1]
    return jnp.where(lax.broadcasted_iota(jnp.int32, (tok, slots), 0) == token, 1.0, 0.0).astype(BF16)


def rows_body(*refs):
    sources, (own, x, g, block), held, sem = refs[:8], refs[8:12], refs[12:20], refs[20]
    copies = [pltpu.make_async_copy(s, h, sem.at[i]) for i, (s, h) in enumerate(zip(sources, held))]
    for copy in copies:
        copy.start()
    tokens, grad_out, token, count, gate, w_gate, w_up, w_down = held
    rows = w_gate.shape[0]
    for i, weight in ((5, w_gate), (6, w_up), (7, w_down)):
        copies[i].wait()
        block[rows * (i - 5) : rows * (i - 4)] = weight[...]
    for i in (2, 3, 4, 0):
        copies[i].wait()
    pick = pick_of(token[...], tokens.shape[0])
    x[...] = dot(pick, tokens[...], FIRST).astype(BF16)
    own[0] = x[...]
    copies[1].wait()
    g[...] = (use_of(gate[...], count[...]) * dot(pick, grad_out[...], FIRST)).astype(BF16)
    own[1] = g[...]


def copies_body(block, copies):
    for i in range(copies.shape[0]):
        copies[i] = block[...]


def products(part, held, weights):
    slots, units = held[0][0].shape[0], weights.shape[2]
    for which, pair in enumerate(held):
        for m in range(3):
            part[slots * which : slots * (which + 1), units * m : units * (m + 1)] = dot(
                pair[m // 2][...], weights[m]
            ).astype(BF16)


def far_products_body(pieces, x0, g0, x1, g1, part, weights):
    rows, cols = pieces.shape[1] // 3, pieces.shape[2]
    for i, (half, place) in enumerate(PIECES):
        for m in range(3):
            weights[m, rows * place : rows * (place + 1), cols * half : cols * (half + 1)] = pieces[
                i, rows * m : rows * (m + 1)
            ]
    products(part, ((x0, g0), (x1, g1)), weights)


def near_products_body(weights, own, core, part):
    products(part, [(held.at[0], held.at[1]) for held in (own, core)], weights)


def act_body(got, theirs, acts):
    total = got[0].astype(F32)
    for i in range(1, got.shape[0]):
        total = total + got[i].astype(F32)
    total = total + theirs[...].astype(F32)
    units = total.shape[1] // 3
    pre_gate, pre_up, grad_hidden = total[:, :units], total[:, units : 2 * units], total[:, 2 * units :]
    sigma = jax.nn.sigmoid(pre_gate)
    back_gate = (grad_hidden * pre_up * sigma * (1.0 + pre_gate * (1.0 - sigma))).astype(BF16)
    back_up = (grad_hidden * pre_gate * sigma).astype(BF16)
    hidden = (pre_gate * sigma * pre_up).astype(BF16)
    for i in range(got.shape[0]):
        acts[i, :, :units] = back_gate
        acts[i, :, units : 2 * units] = back_up
        acts[i, :, 2 * units :] = hidden


def outputs(acts, weights, which):
    units = weights.shape[2]
    if which == 0:
        return dot(acts[:, 2 * units :], weights[2], LAST)
    return dot(acts[:, :units], weights[0], LAST) + dot(acts[:, units : 2 * units], weights[1], LAST)


def outputs_body(acts, weights, mine, send):
    slots = mine.shape[1]
    for which in range(2):
        out = outputs(acts, weights, which)
        mine[which] = out[:slots]
        send[which] = out[slots:].astype(BF16)


def term(acts, held, m):
    units, slots = acts.shape[1] // 3, held[0][0].shape[0]
    cut = slice(units * m, units * (m + 1))
    (a, b) = [held[i][m // 2][...] for i in range(2)]
    return dot(a, acts[:slots, cut], FIRST) + dot(b, acts[slots:, cut], FIRST)


def far_terms_body(acts, x0, g0, x1, g1, terms):
    units = acts.shape[1] // 3
    for m in range(3):
        terms[:, units * m : units * (m + 1)] = term(acts, ((x0, g0), (x1, g1)), m)


def near_terms_body(*refs):
    sources, pieces, held, sem = refs[:4], refs[4], refs[5:9], refs[9]
    copies = [pltpu.make_async_copy(s, h, sem.at[i]) for i, (s, h) in enumerate(zip(sources, held))]
    for copy in copies:
        copy.start()
    acts, own, core, terms = held
    units = terms.shape[1] // 3
    rows, cols = pieces.shape[1] // 3, pieces.shape[2]
    for i in range(3):
        copies[i].wait()
    for m in range(3):
        total = term(acts, [(ref.at[0], ref.at[1]) for ref in (own, core)], m)
        if m == 0:
            copies[3].wait()
        total = (total + terms[:, units * m : units * (m + 1)]).astype(BF16)
        for i, (half, place) in enumerate(PIECES):
            pieces[i, rows * m : rows * (m + 1)] = total[
                rows * place : rows * (place + 1), cols * half : cols * (half + 1)
            ]


def tokens_body(mine, core, chip, token, count, gate, mixed, grad_tokens):
    pick = pick_of(token[...], mixed.shape[0])
    out, back = [mine[i] + core[i].astype(F32) + chip[i].astype(F32) for i in range(2)]
    mixed[...] = dot(pick, (use_of(gate[...], count[...]) * out).astype(BF16)).astype(BF16)
    grad_tokens[...] = dot(pick, back.astype(BF16)).astype(BF16)


def local(tokens, grad_out, slot_token, slot_count, slot_gate, w_gate, w_up, w_down):
    slots, (tok, feat) = slot_token.shape[0], tokens.shape
    rows, cols = w_gate.shape
    units = 2 * cols
    token, gate, count = slot_token[None], slot_gate[None], slot_count[None]
    pick_flops = 4 * slots * tok * feat
    own_shape = (slots, feat)
    own, x, g, block = call(
        rows_body,
        [((2, slots, feat), BF16), (own_shape, BF16), (own_shape, BF16), ((3 * rows, cols), BF16)],
        pick_flops,
        *(tokens, grad_out, token, count, gate, w_gate, w_up, w_down),
        fetch=True,
        grant=60,
    )

    block = lax.ppermute(block, ("wide", "narrow"), SWAP)
    chip_x = lax.ppermute(x, "wide", OTHER_CHIP)
    core_own = lax.ppermute(own, "wide", OTHER_CORE)
    (pieces,) = call(
        copies_body, [((len(PIECES),) + block.shape, BF16)], 0, block, after=(chip_x, core_own)
    )
    pieces = exchange(pieces, "wide", OWNERS)
    chip_g = lax.ppermute(g, "wide", OTHER_CHIP)
    core_x = lax.ppermute(chip_x, "wide", OTHER_CORE)
    core_g = lax.ppermute(chip_g, "wide", OTHER_CORE)
    far = (chip_x, chip_g, core_x, core_g)

    flops = 2 * 3 * 2 * slots * feat * units
    wide_part = ((2 * slots, 3 * units), BF16)
    part_far, weights = call(
        far_products_body, [wide_part, ((3, feat, units), BF16)], flops, pieces, *far
    )
    (part_near,) = call(near_products_body, [wide_part], flops, weights, own, core_own)
    portion = 2 * slots // N_X
    parts = (N_X, portion, 3 * units)

    def narrow_sum(part):
        got = exchange(part.reshape(parts), "narrow", ALONG_X)
        sent = got.astype(F32).sum(axis=0).astype(BF16)
        return got, lax.ppermute(sent, "narrow", OTHER_HALF)

    def activations(got, theirs, after):
        (acts,) = call(
            act_body, [(parts, BF16)], 20 * portion * 3 * units, got, theirs, after=after
        )
        return exchange(acts, "narrow", ALONG_X).reshape(2 * slots, 3 * units)

    got_far, theirs_far = narrow_sum(part_far)
    got_near, theirs_near = narrow_sum(part_near)
    acts_far = activations(got_far, theirs_far, (got_near,))
    acts_near = activations(got_near, theirs_near, (acts_far,))

    out_shapes = [((2, slots, feat), F32), ((2, slots, feat), BF16)]
    chip, send = call(outputs_body, out_shapes, flops, acts_far, weights)
    chip = (chip + lax.ppermute(send, "wide", OTHER_CORE).astype(F32)).astype(BF16)
    chip = lax.ppermute(chip, "wide", OTHER_CHIP)
    (terms,) = call(far_terms_body, [((feat, 3 * units), F32)], flops, acts_far, *far)
    (terms,) = call(
        near_terms_body,
        [(pieces.shape, BF16)],
        flops,
        *(acts_near, own, core_own, terms),
        fetch=True,
    )
    terms = exchange(terms, "wide", OWNERS)
    mine, send = call(outputs_body, out_shapes, flops, acts_near, weights)
    core = lax.ppermute(send, "wide", OTHER_CORE)
    grads = terms.astype(F32).sum(axis=0).astype(BF16)
    grads = lax.ppermute(grads, ("wide", "narrow"), SWAP_BACK).astype(F32)
    mixed, grad_tokens = call(
        tokens_body, [((tok, feat), BF16)] * 2, pick_flops, *(mine, core, chip, token, count, gate)
    )
    return mixed, grad_tokens, grads[:rows], grads[rows : 2 * rows], grads[2 * rows :]


def solution(mesh):
    both = P("wide", "narrow")
    in_specs = (both, both, P("wide"), P("wide"), P("wide"), both, both, both)
    return jax.shard_map(
        local, mesh=mesh, in_specs=in_specs, out_specs=(both,) * 5, check_vma=False
    )
```

```python
import jax
import jax.numpy as jnp
from jax import lax
from jax.experimental import pallas as pl
from jax.experimental.pallas import tpu as pltpu
from jax.sharding import PartitionSpec as P

N_Y, N_Z, N_CORE, N_X = 8, 4, 2, 4
N_WIDE, N_NARROW = N_Y * N_Z * N_CORE, 2 * N_X
F32, BF16 = jnp.float32, jnp.bfloat16
FIRST, LAST, PLAIN = ((0,), (0,)), ((1,), (1,)), ((1,), (0,))


def wide_index(y, z, core):
    return (y * N_Z + z) * N_CORE + core


def swap_pairs():
    pairs = []
    for y in range(N_Y):
        for z in range(N_Z):
            for core in range(N_CORE):
                for n in range(N_NARROW):
                    to = wide_index(y // 2 * 2 + core, z, n % 2)
                    pairs.append((wide_index(y, z, core) * N_NARROW + n, to * N_NARROW + n // 2 * 2 + y % 2))
    return pairs


SWAP = swap_pairs()
SWAP_BACK = [(b, a) for a, b in SWAP]
OTHER_CORE = [(w, w ^ 1) for w in range(N_WIDE)]
OTHER_HALF = [(n, n ^ 1) for n in range(N_NARROW)]
OWNERS = [[wide_index(y, z, core) for y in range(N_Y) for z in range(N_Z)] for core in range(N_CORE)]


def shift_x(by):
    return [(n, (n + 2 * by) % N_NARROW) for n in range(N_NARROW)]


def dot(a, b, dims=PLAIN):
    return lax.dot_general(a, b, (dims, ((), ())), preferred_element_type=F32)


def call(body, outs, flops, where, *args):
    size = sum(a.size * a.dtype.itemsize for a in args)
    count = len(args)

    def inner(where_ref, *refs):
        sources, results = refs[:count], refs[count : count + len(outs)]
        held, sem = refs[count + len(outs) : -1], refs[-1]
        copies = [
            pltpu.make_async_copy(s, h, sem.at[i]) for i, (s, h) in enumerate(zip(sources, held))
        ]
        for copy in copies:
            copy.start()
        here = set()

        def get(i):
            if i not in here:
                here.add(i)
                copies[i].wait()
            return held[i]

        body(where_ref, get, *results)

    return pl.pallas_call(
        inner,
        out_shape=[jax.ShapeDtypeStruct(shape, kind) for shape, kind in outs],
        in_specs=[pl.BlockSpec(memory_space=pltpu.SMEM)]
        + [pl.BlockSpec(memory_space=pl.ANY)] * count,
        out_specs=[pl.BlockSpec(memory_space=pltpu.VMEM)] * len(outs),
        scratch_shapes=[pltpu.VMEM(a.shape, a.dtype) for a in args]
        + [pltpu.SemaphoreType.DMA((count,))],
        compiler_params=pltpu.CompilerParams(vmem_limit_bytes=60 * 1024 * 1024),
        cost_estimate=pl.CostEstimate(flops=flops, bytes_accessed=size, transcendentals=0),
    )(where, *args)


def use_of(gate, count):
    slots = gate.shape[1]
    lane = lax.broadcasted_iota(jnp.int32, (1, slots), 1)
    use = jnp.where(lane < count, gate, 0.0)
    square = lax.broadcasted_iota(jnp.int32, (slots, slots), 0) == lax.broadcasted_iota(
        jnp.int32, (slots, slots), 1
    )
    return jnp.sum(jnp.where(square, use, 0.0), axis=1, keepdims=True)


def pick_of(token, tok):
    slots = token.shape[1]
    return jnp.where(lax.broadcasted_iota(jnp.int32, (tok, slots), 0) == token, 1.0, 0.0).astype(BF16)


def rows_body(where, get, own, block):
    rows = block.shape[0] // 3
    for i in range(3):
        block[rows * i : rows * (i + 1)] = get(5 + i)[...]
    token, count, gate, tokens = get(2), get(3), get(4), get(0)
    pick = pick_of(token[...], tokens.shape[0])
    own[0] = dot(pick, tokens[...], FIRST).astype(BF16)
    own[1] = (use_of(gate[...], count[...]) * dot(pick, get(1)[...], FIRST)).astype(BF16)


def turn(where, step, size):
    return pl.multiple_of(lax.rem(where[0] + step, N_X) * size, size)


def products_body(where, get, sent, kept, both, down):
    pieces = get(0)
    rows, cols = pieces.shape[1] // 3, pieces.shape[2]
    for i in range(pieces.shape[0]):
        y, z = divmod(i, N_Z)
        at = slice((y // 2 * 8 + z * 2 + y % 2) * rows, (y // 2 * 8 + z * 2 + y % 2 + 1) * rows)
        both[at, :cols] = pieces[i, :rows]
        both[at, cols:] = pieces[i, rows : 2 * rows]
        down[at] = pieces[i, 2 * rows :]
    slots, feat = get(1).shape[1:]
    for who in range(2):
        pre, back = 0.0, 0.0
        for step in range(N_X):
            x = get(1 + who * N_X + step)
            at = pl.ds(turn(where, step, feat), feat)
            pre = pre + dot(x[0], both[at])
            back = back + dot(x[1], down[at])
        at = slice(slots * who, slots * (who + 1))
        kept[at, : 2 * cols] = pre
        kept[at, 2 * cols :] = back
        sent[at, : 2 * cols] = pre.astype(BF16)
        sent[at, 2 * cols :] = back.astype(BF16)


def outputs_body(where, get, acts, mine, send):
    kept, theirs, both, down = [get(i) for i in range(4)]
    total = kept[...] + theirs[...].astype(F32)
    units = total.shape[1] // 3
    pre_gate, pre_up, grad_hidden = total[:, :units], total[:, units : 2 * units], total[:, 2 * units :]
    sigma = jax.nn.sigmoid(pre_gate)
    acts[:, :units] = (
        grad_hidden * pre_up * sigma * (1.0 + pre_gate * (1.0 - sigma))
    ).astype(BF16)
    acts[:, units : 2 * units] = (grad_hidden * pre_gate * sigma).astype(BF16)
    acts[:, 2 * units :] = (pre_gate * sigma * pre_up).astype(BF16)
    slots, feat = mine.shape[2:]
    for step in range(N_X):
        at = pl.ds(turn(where, step, feat), feat)
        for which, out in enumerate(
            (dot(acts[:, 2 * units :], down[at], LAST), dot(acts[:, : 2 * units], both[at], LAST))
        ):
            mine[step, which] = out[:slots].astype(BF16)
            send[step, which] = out[slots:].astype(BF16)


def terms_body(where, get, pieces):
    acts = get(0)
    rows, cols = pieces.shape[1] // 3, pieces.shape[2]
    slots = acts.shape[0] // 2
    for step in range(N_X):
        near, core = get(1 + step), get(1 + N_X + step)
        both = dot(near[0], acts[:slots, : 2 * cols], FIRST)
        both = (both + dot(core[0], acts[slots:, : 2 * cols], FIRST)).astype(BF16)
        down = dot(near[1], acts[:slots, 2 * cols :], FIRST)
        down = (down + dot(core[1], acts[slots:, 2 * cols :], FIRST)).astype(BF16)
        first = turn(where, step, 2 * N_Z)
        for i in range(2 * N_Z):
            y, z = divmod(i, N_Z)
            at = slice((z * 2 + y) * rows, (z * 2 + y + 1) * rows)
            pieces[first + i, :rows] = both[at, :cols]
            pieces[first + i, rows : 2 * rows] = both[at, cols:]
            pieces[first + i, 2 * rows :] = down[at]


def sums_body(where, get, *sums):
    for step in range(N_X):
        sums[step][...] = (get(0)[step].astype(F32) + get(1)[step].astype(F32)).astype(BF16)


def tokens_body(where, get, mixed, grad_tokens):
    token, count, gate = get(0), get(1), get(2)
    pick = pick_of(token[...], mixed.shape[0])
    out, back = [sum(get(3 + step)[i].astype(F32) for step in range(N_X)) for i in range(2)]
    mixed[...] = dot(pick, (use_of(gate[...], count[...]) * out).astype(BF16)).astype(BF16)
    grad_tokens[...] = dot(pick, back.astype(BF16)).astype(BF16)


def local(tokens, grad_out, slot_token, slot_count, slot_gate, w_gate, w_up, w_down):
    slots, (tok, feat) = slot_token.shape[0], tokens.shape
    rows, cols = w_gate.shape
    token, gate, count = slot_token[None], slot_gate[None], slot_count[None]
    where = (lax.axis_index("narrow") // 2).astype(jnp.int32)[None]
    pick_flops = 4 * slots * tok * feat
    own, block = call(
        rows_body,
        [((2, slots, feat), BF16), ((3 * rows, cols), BF16)],
        pick_flops,
        where,
        *(tokens, grad_out, token, count, gate, w_gate, w_up, w_down),
    )

    block = lax.ppermute(block, ("wide", "narrow"), SWAP)
    pieces = jnp.broadcast_to(block[None], (len(OWNERS[0]),) + block.shape)
    pieces = lax.all_to_all(pieces, "wide", 0, 0, axis_index_groups=OWNERS)
    near = [own] + [lax.ppermute(own, "narrow", shift_x(-step)) for step in range(1, N_X)]
    core = [lax.ppermute(held, "wide", OTHER_CORE) for held in near]

    flops = 2 * 3 * 2 * slots * N_X * feat * cols
    part = (2 * slots, 3 * cols)
    sent, kept, both, down = call(
        products_body,
        [(part, BF16), (part, F32), ((N_X * feat, 2 * cols), BF16), ((N_X * feat, cols), BF16)],
        flops,
        where,
        *(pieces, *near, *core),
    )
    theirs = lax.ppermute(sent, "narrow", OTHER_HALF)

    every = ((N_X, 2, slots, feat), BF16)
    acts, mine, send = call(
        outputs_body, [(part, BF16), every, every], flops, where, kept, theirs, both, down
    )
    (terms,) = call(terms_body, [(pieces.shape, BF16)], flops, where, acts, *near, *core)

    got = lax.ppermute(send, "wide", OTHER_CORE)
    sums = call(sums_body, [((2, slots, feat), BF16)] * N_X, 0, where, mine, got)
    home = [sums[0]] + [
        lax.ppermute(sums[step], "narrow", shift_x(step)) for step in range(1, N_X)
    ]
    mixed, grad_tokens = call(
        tokens_body, [((tok, feat), BF16)] * 2, pick_flops, where, token, count, gate, *home
    )

    terms = lax.all_to_all(terms, "wide", 0, 0, axis_index_groups=OWNERS)
    grads = terms.astype(F32).sum(axis=0).astype(BF16)
    grads = lax.ppermute(grads, ("wide", "narrow"), SWAP_BACK).astype(F32)
    return mixed, grad_tokens, grads[:rows], grads[rows : 2 * rows], grads[2 * rows :]


def solution(mesh):
    both = P("wide", "narrow")
    in_specs = (both, both, P("wide"), P("wide"), P("wide"), both, both, both)
    return jax.shard_map(
        local, mesh=mesh, in_specs=in_specs, out_specs=(both,) * 5, check_vma=False
    )
```

```python
import jax
import jax.numpy as jnp
from jax import lax
from jax.experimental import pallas as pl
from jax.experimental.pallas import tpu as pltpu
from jax.sharding import PartitionSpec as P

N_Y, N_Z, N_CORE, N_X = 8, 4, 2, 4
N_WIDE, N_NARROW = N_Y * N_Z * N_CORE, 2 * N_X
F32, BF16 = jnp.float32, jnp.bfloat16
FIRST, LAST, PLAIN = ((0,), (0,)), ((1,), (1,)), ((1,), (0,))


def wide_index(y, z, core):
    return (y * N_Z + z) * N_CORE + core


def swap_pairs():
    pairs = []
    for y in range(N_Y):
        for z in range(N_Z):
            for core in range(N_CORE):
                for n in range(N_NARROW):
                    to = wide_index(y // 2 * 2 + core, z, n % 2)
                    pairs.append((wide_index(y, z, core) * N_NARROW + n, to * N_NARROW + n // 2 * 2 + y % 2))
    return pairs


SWAP = swap_pairs()
SWAP_BACK = [(b, a) for a, b in SWAP]
OTHER_CORE = [(w, w ^ 1) for w in range(N_WIDE)]
OTHER_HALF = [(n, n ^ 1) for n in range(N_NARROW)]
OWNERS = [[wide_index(y, z, core) for y in range(N_Y) for z in range(N_Z)] for core in range(N_CORE)]


def shift_x(by):
    return [(n, (n + 2 * by) % N_NARROW) for n in range(N_NARROW)]


def dot(a, b, dims=PLAIN):
    return lax.dot_general(a, b, (dims, ((), ())), preferred_element_type=F32)


def call(body, outs, flops, where, *args):
    size = sum(a.size * a.dtype.itemsize for a in args)
    count, results = len(args), len(outs)
    most = N_X * results

    def inner(where_ref, *refs):
        sources, targets = refs[:count], refs[count : count + results]
        held, made = refs[count + results : -2 - results], refs[-2 - results : -2]
        sem, out_sem = refs[-2:]
        copies = [
            pltpu.make_async_copy(s, h, sem.at[i]) for i, (s, h) in enumerate(zip(sources, held))
        ]
        for copy in copies:
            copy.start()
        here, leaving = set(), []

        def get(i):
            if i not in here:
                here.add(i)
                copies[i].wait()
            return held[i]

        def put(i, at=slice(None)):
            copy = pltpu.make_async_copy(made[i].at[at], targets[i].at[at], out_sem.at[len(leaving)])
            copy.start()
            leaving.append(copy)
            whole.discard(i)

        whole = set(range(results))
        body(where_ref, get, put, *made)
        for i in sorted(whole):
            put(i)
        for i in range(count):
            get(i)
        for copy in leaving:
            copy.wait()

    shapes = [jax.ShapeDtypeStruct(shape, kind) for shape, kind in outs]
    return pl.pallas_call(
        inner,
        out_shape=shapes,
        in_specs=[pl.BlockSpec(memory_space=pltpu.SMEM)]
        + [pl.BlockSpec(memory_space=pl.ANY)] * count,
        out_specs=[pl.BlockSpec(memory_space=pl.ANY)] * results,
        scratch_shapes=[pltpu.VMEM(a.shape, a.dtype) for a in (*args, *shapes)]
        + [pltpu.SemaphoreType.DMA((count,)), pltpu.SemaphoreType.DMA((most,))],
        compiler_params=pltpu.CompilerParams(vmem_limit_bytes=60 * 1024 * 1024),
        cost_estimate=pl.CostEstimate(flops=flops, bytes_accessed=size, transcendentals=0),
    )(where, *args)


def use_of(gate, count):
    slots = gate.shape[1]
    lane = lax.broadcasted_iota(jnp.int32, (1, slots), 1)
    use = jnp.where(lane < count, gate, 0.0)
    square = lax.broadcasted_iota(jnp.int32, (slots, slots), 0) == lax.broadcasted_iota(
        jnp.int32, (slots, slots), 1
    )
    return jnp.sum(jnp.where(square, use, 0.0), axis=1, keepdims=True)


def pick_of(token, tok):
    slots = token.shape[1]
    return jnp.where(lax.broadcasted_iota(jnp.int32, (tok, slots), 0) == token, 1.0, 0.0).astype(BF16)


def block_body(where, get, put, block):
    rows = block.shape[0] // 3
    for i in range(3):
        block[rows * i : rows * (i + 1)] = get(i)[...]


def rows_body(where, get, put, own):
    token, count, gate, tokens = get(2), get(3), get(4), get(0)
    pick = pick_of(token[...], tokens.shape[0])
    own[0] = dot(pick, tokens[...], FIRST).astype(BF16)
    put(0, pl.ds(0, 1))
    own[1] = (use_of(gate[...], count[...]) * dot(pick, get(1)[...], FIRST)).astype(BF16)
    put(0, pl.ds(1, 1))


def turned_body(where, get, put, *turned):
    slots = get(0).shape[1]
    for step in range(N_X):
        for who in range(2):
            for which in range(2):
                turned[step][which, :, slots * who : slots * (who + 1)] = get(who * N_X + step)[which].T
        put(step)


def turn(where, step, size):
    return pl.multiple_of(lax.rem(where[0] + step, N_X) * size, size)


def assemble(pieces, both, down):
    rows, cols = pieces.shape[1] // 3, pieces.shape[2]
    for i in range(pieces.shape[0]):
        y, z = divmod(i, N_Z)
        place = y // 2 * 8 + z * 2 + y % 2
        at = slice(place * rows, (place + 1) * rows)
        both[at, :cols] = pieces[i, :rows]
        both[at, cols:] = pieces[i, rows : 2 * rows]
        down[at] = pieces[i, 2 * rows :]


def products_body(where, get, put, part, both, down):
    assemble(get(0), both, down)
    put(1)
    put(2)
    cols = down.shape[1]
    slots, feat = get(1).shape[1:]
    for who in range(2):
        pre, back = 0.0, 0.0
        for step in range(N_X):
            x = get(1 + who * N_X + step)
            at = pl.ds(turn(where, step, feat), feat)
            pre = pre + dot(x[0], both[at])
            back = back + dot(x[1], down[at])
        at = slice(slots * who, slots * (who + 1))
        part[at, : 2 * cols] = pre.astype(BF16)
        part[at, 2 * cols :] = back.astype(BF16)
        put(0, pl.ds(slots * who, slots))


def terms_body(where, get, put, pieces, acts):
    total = get(0)[...].astype(F32) + get(1)[...].astype(F32)
    units = total.shape[1] // 3
    pre_gate, pre_up, grad_hidden = total[:, :units], total[:, units : 2 * units], total[:, 2 * units :]
    sigma = jax.nn.sigmoid(pre_gate)
    acts[:, :units] = (
        grad_hidden * pre_up * sigma * (1.0 + pre_gate * (1.0 - sigma))
    ).astype(BF16)
    acts[:, units : 2 * units] = (grad_hidden * pre_gate * sigma).astype(BF16)
    acts[:, 2 * units :] = (pre_gate * sigma * pre_up).astype(BF16)
    put(1)
    rows = pieces.shape[1] // 3
    for step in range(N_X):
        turned = get(2 + step)
        both = dot(turned[0], acts[:, : 2 * units]).astype(BF16)
        down = dot(turned[1], acts[:, 2 * units :]).astype(BF16)
        first = turn(where, step, 2 * N_Z)
        for i in range(2 * N_Z):
            y, z = divmod(i, N_Z)
            at = slice((z * 2 + y) * rows, (z * 2 + y + 1) * rows)
            pieces[first + i, :rows] = both[at, :units]
            pieces[first + i, rows : 2 * rows] = both[at, units:]
            pieces[first + i, 2 * rows :] = down[at]
        put(0, pl.ds(first, 2 * N_Z))


def outputs_body(where, get, put, send, mine):
    acts, both, down = [get(i) for i in range(3)]
    units = acts.shape[1] // 3
    slots, feat = mine.shape[2:]
    for step in (2, 1, 3, 0):
        at = pl.ds(turn(where, step, feat), feat)
        for which, out in enumerate(
            (dot(acts[:, 2 * units :], down[at], LAST), dot(acts[:, : 2 * units], both[at], LAST))
        ):
            mine[step, which] = out[:slots].astype(BF16)
            send[step, which] = out[slots:].astype(BF16)
        put(0, pl.ds(step, 1))
        put(1, pl.ds(step, 1))


def tokens_body(where, get, put, mixed, grad_tokens):
    token, count, gate = get(0), get(1), get(2)
    pick = pick_of(token[...], mixed.shape[0])
    out, back = [sum(get(3 + step)[i].astype(F32) for step in range(N_X)) for i in range(2)]
    mixed[...] = dot(pick, (use_of(gate[...], count[...]) * out).astype(BF16)).astype(BF16)
    put(0)
    grad_tokens[...] = dot(pick, back.astype(BF16)).astype(BF16)


def local(tokens, grad_out, slot_token, slot_count, slot_gate, w_gate, w_up, w_down):
    slots, (tok, feat) = slot_token.shape[0], tokens.shape
    rows, cols = w_gate.shape
    token, gate, count = slot_token[None], slot_gate[None], slot_count[None]
    where = (lax.axis_index("narrow") // 2).astype(jnp.int32)[None]
    pick_flops = 4 * slots * tok * feat

    (block,) = call(block_body, [((3 * rows, cols), BF16)], 0, where, w_gate, w_up, w_down)
    block = lax.ppermute(block, ("wide", "narrow"), SWAP)
    pieces = jnp.broadcast_to(block[None], (len(OWNERS[0]),) + block.shape)
    pieces = lax.all_to_all(pieces, "wide", 0, 0, axis_index_groups=OWNERS)
    (own,) = call(
        rows_body,
        [((2, slots, feat), BF16)],
        pick_flops,
        where,
        *(tokens, grad_out, token, count, gate),
    )
    near = [own] + [lax.ppermute(own, "narrow", shift_x(-step)) for step in range(1, N_X)]
    core = [lax.ppermute(held, "wide", OTHER_CORE) for held in near]
    turned = call(
        turned_body, [((2, feat, 2 * slots), BF16)] * N_X, pick_flops, where, *near, *core
    )

    flops = 2 * 3 * 2 * slots * N_X * feat * cols
    part = ((2 * slots, 3 * cols), BF16)
    sent, both, down = call(
        products_body,
        [part, ((N_X * feat, 2 * cols), BF16), ((N_X * feat, cols), BF16)],
        flops,
        where,
        *(pieces, *near, *core),
    )
    theirs = lax.ppermute(sent, "narrow", OTHER_HALF)
    terms, acts = call(
        terms_body,
        [(pieces.shape, BF16), part],
        flops,
        where,
        *(sent, theirs, *turned),
    )

    terms = lax.all_to_all(terms, "wide", 0, 0, axis_index_groups=OWNERS)
    grads = terms.astype(F32).sum(axis=0).astype(BF16)
    grads = lax.ppermute(grads, ("wide", "narrow"), SWAP_BACK).astype(F32)

    every = ((N_X, 2, slots, feat), BF16)
    send, mine = call(outputs_body, [every, every], flops, where, acts, both, down)
    got = lax.ppermute(send, "wide", OTHER_CORE)
    sums = [(mine[step].astype(F32) + got[step].astype(F32)).astype(BF16) for step in range(N_X)]
    home = [sums[0]] + [
        lax.ppermute(sums[step], "narrow", shift_x(step)) for step in range(1, N_X)
    ]
    mixed, grad_tokens = call(
        tokens_body, [((tok, feat), BF16)] * 2, pick_flops, where, token, count, gate, *home
    )
    return mixed, grad_tokens, grads[:rows], grads[rows : 2 * rows], grads[2 * rows :]


def solution(mesh):
    both = P("wide", "narrow")
    in_specs = (both, both, P("wide"), P("wide"), P("wide"), both, both, both)
    return jax.shard_map(
        local, mesh=mesh, in_specs=in_specs, out_specs=(both,) * 5, check_vma=False
    )
```

```python
import jax
import jax.numpy as jnp
from jax import lax
from jax.experimental import pallas as pl
from jax.experimental.pallas import tpu as pltpu
from jax.sharding import PartitionSpec as P

N_Y, N_Z, N_CORE, N_X = 8, 4, 2, 4
N_WIDE, N_NARROW = N_Y * N_Z * N_CORE, 2 * N_X
F32, BF16 = jnp.float32, jnp.bfloat16
FIRST, LAST, PLAIN = ((0,), (0,)), ((1,), (1,)), ((1,), (0,))


def wide_index(y, z, core):
    return (y * N_Z + z) * N_CORE + core


def swap_pairs():
    pairs = []
    for y in range(N_Y):
        for z in range(N_Z):
            for core in range(N_CORE):
                for n in range(N_NARROW):
                    to = wide_index(y // 2 * 2 + core, z, n % 2)
                    pairs.append((wide_index(y, z, core) * N_NARROW + n, to * N_NARROW + n // 2 * 2 + y % 2))
    return pairs


SWAP = swap_pairs()
SWAP_BACK = [(b, a) for a, b in SWAP]
OTHER_CORE = [(w, w ^ 1) for w in range(N_WIDE)]
OTHER_HALF = [(n, n ^ 1) for n in range(N_NARROW)]
OWNERS = [[wide_index(y, z, core) for y in range(N_Y) for z in range(N_Z)] for core in range(N_CORE)]


def shift_x(by):
    return [(n, (n + 2 * by) % N_NARROW) for n in range(N_NARROW)]


def dot(a, b, dims=PLAIN):
    return lax.dot_general(a, b, (dims, ((), ())), preferred_element_type=F32)


def call(body, outs, flops, where, *args, after=(), grant=60):
    size = sum(a.size * a.dtype.itemsize for a in args)
    count, results = len(args), len(outs)
    most = N_X * results

    def inner(where_ref, *refs):
        sources, refs = refs[:count], refs[count + len(after) :]
        targets, held = refs[:results], refs[results : results + count]
        made, (sem, out_sem) = refs[results + count : -2], refs[-2:]
        copies = [
            pltpu.make_async_copy(s, h, sem.at[i]) for i, (s, h) in enumerate(zip(sources, held))
        ]
        for copy in copies:
            copy.start()
        here, leaving = set(), []

        def get(i):
            if i not in here:
                here.add(i)
                copies[i].wait()
            return held[i]

        def put(i, at=slice(None)):
            copy = pltpu.make_async_copy(made[i].at[at], targets[i].at[at], out_sem.at[len(leaving)])
            copy.start()
            leaving.append(copy)
            whole.discard(i)

        whole = set(range(results))
        body(where_ref, get, put, *made)
        for i in sorted(whole):
            put(i)
        for i in range(count):
            get(i)
        for copy in leaving:
            copy.wait()

    shapes = [jax.ShapeDtypeStruct(shape, kind) for shape, kind in outs]
    return pl.pallas_call(
        inner,
        out_shape=shapes,
        in_specs=[pl.BlockSpec(memory_space=pltpu.SMEM)]
        + [pl.BlockSpec(memory_space=pl.ANY)] * (count + len(after)),
        out_specs=[pl.BlockSpec(memory_space=pl.ANY)] * results,
        scratch_shapes=[pltpu.VMEM(a.shape, a.dtype) for a in (*args, *shapes)]
        + [pltpu.SemaphoreType.DMA((count,)), pltpu.SemaphoreType.DMA((most,))],
        compiler_params=pltpu.CompilerParams(vmem_limit_bytes=grant * 1024 * 1024),
        cost_estimate=pl.CostEstimate(flops=flops, bytes_accessed=size, transcendentals=0),
    )(where, *args, *after)


def use_of(gate, count):
    slots = gate.shape[1]
    lane = lax.broadcasted_iota(jnp.int32, (1, slots), 1)
    use = jnp.where(lane < count, gate, 0.0)
    square = lax.broadcasted_iota(jnp.int32, (slots, slots), 0) == lax.broadcasted_iota(
        jnp.int32, (slots, slots), 1
    )
    return jnp.sum(jnp.where(square, use, 0.0), axis=1, keepdims=True)


def pick_of(token, tok):
    slots = token.shape[1]
    return jnp.where(lax.broadcasted_iota(jnp.int32, (tok, slots), 0) == token, 1.0, 0.0).astype(BF16)


def block_body(where, get, put, block):
    rows = block.shape[0] // 3
    for i in range(3):
        block[rows * i : rows * (i + 1)] = get(i)[...]


def rows_body(where, get, put, own):
    token, count, gate, tokens = get(2), get(3), get(4), get(0)
    pick = pick_of(token[...], tokens.shape[0])
    own[0] = dot(pick, tokens[...], FIRST).astype(BF16)
    put(0, pl.ds(0, 1))
    own[1] = (use_of(gate[...], count[...]) * dot(pick, get(1)[...], FIRST)).astype(BF16)
    put(0, pl.ds(1, 1))


def turned_body(where, get, put, *turned):
    slots = get(0).shape[1]
    for step in range(N_X):
        for who in range(2):
            for which in range(2):
                turned[step][which, :, slots * who : slots * (who + 1)] = get(who * N_X + step)[which].T
        put(step)


def turn(where, step, size):
    return pl.multiple_of(lax.rem(where[0] + step, N_X) * size, size)


def products_body(where, get, put, part, weights):
    pieces = get(0)
    rows, cols = pieces.shape[1] // 3, pieces.shape[2]
    for i in range(pieces.shape[0]):
        y, z = divmod(i, N_Z)
        place = y // 2 * 8 + z * 2 + y % 2
        for m in range(3):
            weights[place * rows : (place + 1) * rows, cols * m : cols * (m + 1)] = pieces[
                i, rows * m : rows * (m + 1)
            ]
    put(1)
    slots, feat = get(1).shape[1:]
    for who in range(2):
        pre, back = 0.0, 0.0
        for step in range(N_X):
            x = get(1 + who * N_X + step)
            at = pl.ds(turn(where, step, feat), feat)
            pre = pre + dot(x[0], weights[at, : 2 * cols])
            back = back + dot(x[1], weights[at, 2 * cols :])
        at = slice(slots * who, slots * (who + 1))
        part[at, : 2 * cols] = pre.astype(BF16)
        part[at, 2 * cols :] = back.astype(BF16)
        put(0, pl.ds(slots * who, slots))


def terms_body(where, get, put, pieces, acts, send):
    total = get(0)[...].astype(F32) + get(1)[...].astype(F32)
    units = total.shape[1] // 3
    pre_gate, pre_up, grad_hidden = total[:, :units], total[:, units : 2 * units], total[:, 2 * units :]
    sigma = jax.nn.sigmoid(pre_gate)
    acts[:, :units] = (
        grad_hidden * pre_up * sigma * (1.0 + pre_gate * (1.0 - sigma))
    ).astype(BF16)
    acts[:, units : 2 * units] = (grad_hidden * pre_gate * sigma).astype(BF16)
    acts[:, 2 * units :] = (pre_gate * sigma * pre_up).astype(BF16)
    send[...] = acts[send.shape[0] :]
    put(1)
    put(2)
    rows = pieces.shape[1] // 3
    for step in range(N_X):
        turned = get(2 + step)
        both = dot(turned[0], acts[:, : 2 * units]).astype(BF16)
        down = dot(turned[1], acts[:, 2 * units :]).astype(BF16)
        first = turn(where, step, 2 * N_Z)
        for i in range(2 * N_Z):
            y, z = divmod(i, N_Z)
            at = slice((z * 2 + y) * rows, (z * 2 + y + 1) * rows)
            pieces[first + i, :rows] = both[at, :units]
            pieces[first + i, rows : 2 * rows] = both[at, units:]
            pieces[first + i, 2 * rows :] = down[at]
        put(0, pl.ds(first, 2 * N_Z))


def outputs_body(where, get, put, *outs):
    slots, feat = outs[0].shape[1:]
    cols = get(1).shape[1] // 3
    for step in (2, 3, 1, 0):
        at = pl.ds(turn(where, step, feat), feat)
        out, back = 0.0, 0.0
        for who in range(2):
            acts, weights = get(2 * who), get(2 * who + 1)
            out = out + dot(acts[:slots, 2 * cols :], weights[at, 2 * cols :], LAST)
            back = back + dot(acts[:slots, : 2 * cols], weights[at, : 2 * cols], LAST)
        outs[step][0] = out.astype(BF16)
        outs[step][1] = back.astype(BF16)
        put(step)


def tokens_body(where, get, put, mixed, grad_tokens):
    token, count, gate = get(0), get(1), get(2)
    pick = pick_of(token[...], mixed.shape[0])
    out, back = [sum(get(3 + step)[i].astype(F32) for step in range(N_X)) for i in range(2)]
    mixed[...] = dot(pick, (use_of(gate[...], count[...]) * out).astype(BF16)).astype(BF16)
    put(0)
    grad_tokens[...] = dot(pick, back.astype(BF16)).astype(BF16)


def local(tokens, grad_out, slot_token, slot_count, slot_gate, w_gate, w_up, w_down):
    slots, (tok, feat) = slot_token.shape[0], tokens.shape
    rows, cols = w_gate.shape
    token, gate, count = slot_token[None], slot_gate[None], slot_count[None]
    where = (lax.axis_index("narrow") // 2).astype(jnp.int32)[None]
    pick_flops = 4 * slots * tok * feat

    (block,) = call(block_body, [((3 * rows, cols), BF16)], 0, where, w_gate, w_up, w_down)
    block = lax.ppermute(block, ("wide", "narrow"), SWAP)
    pieces = jnp.broadcast_to(block[None], (len(OWNERS[0]),) + block.shape)
    pieces = lax.all_to_all(pieces, "wide", 0, 0, axis_index_groups=OWNERS)
    (own,) = call(
        rows_body,
        [((2, slots, feat), BF16)],
        pick_flops,
        where,
        *(tokens, grad_out, token, count, gate),
    )
    near = {step: lax.ppermute(own, "narrow", shift_x(-step)) for step in (1, 3, 2)}
    near = [own] + [near[step] for step in range(1, N_X)]
    core = [lax.ppermute(held, "wide", OTHER_CORE) for held in near]
    turned = call(
        turned_body, [((2, feat, 2 * slots), BF16)] * N_X, pick_flops, where, *near, *core
    )

    flops = 2 * 3 * 2 * slots * N_X * feat * cols
    part = ((2 * slots, 3 * cols), BF16)
    sent, weights = call(
        products_body,
        [part, ((N_X * feat, 3 * cols), BF16)],
        flops,
        where,
        *(pieces, *near, *core),
    )
    theirs = lax.ppermute(sent, "narrow", OTHER_HALF)
    terms, acts, send = call(
        terms_body,
        [(pieces.shape, BF16), part, ((slots, 3 * cols), BF16)],
        flops,
        where,
        *(sent, theirs, *turned),
    )

    terms = lax.all_to_all(terms, "wide", 0, 0, axis_index_groups=OWNERS)
    grads = terms.astype(F32).sum(axis=0).astype(BF16)
    grads = lax.ppermute(grads, ("wide", "narrow"), SWAP_BACK).astype(F32)

    got = lax.ppermute(send, "wide", OTHER_CORE)
    core_weights = lax.ppermute(weights, "wide", OTHER_CORE)
    outs = call(
        outputs_body,
        [((2, slots, feat), BF16)] * N_X,
        flops,
        where,
        *(acts, weights, got, core_weights),
    )
    home = {step: lax.ppermute(outs[step], "narrow", shift_x(step)) for step in (1, 3, 2)}
    home = [outs[0]] + [home[step] for step in range(1, N_X)]
    mixed, grad_tokens = call(
        tokens_body, [((tok, feat), BF16)] * 2, pick_flops, where, token, count, gate, *home
    )
    return mixed, grad_tokens, grads[:rows], grads[rows : 2 * rows], grads[2 * rows :]


def solution(mesh):
    both = P("wide", "narrow")
    in_specs = (both, both, P("wide"), P("wide"), P("wide"), both, both, both)
    return jax.shard_map(
        local, mesh=mesh, in_specs=in_specs, out_specs=(both,) * 5, check_vma=False
    )
```

```python
import jax
import jax.numpy as jnp
from jax import lax
from jax.experimental import pallas as pl
from jax.experimental.pallas import tpu as pltpu
from jax.sharding import PartitionSpec as P

TERMS = 2 * 10**10
N_Y, N_Z, N_CORE, N_X = 8, 4, 2, 4
N_WIDE, N_NARROW = N_Y * N_Z * N_CORE, 2 * N_X
F32, BF16 = jnp.float32, jnp.bfloat16
FIRST, LAST, PLAIN = ((0,), (0,)), ((1,), (1,)), ((1,), (0,))


def wide_index(y, z, core):
    return (y * N_Z + z) * N_CORE + core


def swap_pairs():
    pairs = []
    for y in range(N_Y):
        for z in range(N_Z):
            for core in range(N_CORE):
                for n in range(N_NARROW):
                    to = wide_index(y // 2 * 2 + core, z, n % 2)
                    pairs.append((wide_index(y, z, core) * N_NARROW + n, to * N_NARROW + n // 2 * 2 + y % 2))
    return pairs


SWAP = swap_pairs()
SWAP_BACK = [(b, a) for a, b in SWAP]
OTHER_CORE = [(w, w ^ 1) for w in range(N_WIDE)]
OTHER_HALF = [(n, n ^ 1) for n in range(N_NARROW)]
OWNERS = [[wide_index(y, z, core) for y in range(N_Y) for z in range(N_Z)] for core in range(N_CORE)]


def shift_x(by):
    return [(n, (n + 2 * by) % N_NARROW) for n in range(N_NARROW)]


def dot(a, b, dims=PLAIN):
    return lax.dot_general(a, b, (dims, ((), ())), preferred_element_type=F32)


def turn(where, step, size):
    return pl.multiple_of(lax.rem(where[0] + step, N_X) * size, size)


def call(body, outs, flops, where, *args, after=(), grant=60, direct=False, keep=False):
    entries = [a if isinstance(a, list) else [a] for a in args]
    flat = [a for entry in entries for a in entry]
    size = sum(a.size * a.dtype.itemsize for a in flat)
    count, results = len(flat), len(outs)
    most = N_X * results

    def shape_of(entry):
        first, rows, *rest = entry[0].shape if len(entry) > 1 else (0, 0)
        return (first, rows * len(entry), *rest) if len(entry) > 1 else entry[0].shape

    def inner(where_ref, *refs):
        sources, refs = refs[:count], refs[count + len(after) :]
        targets, held = refs[:results], refs[results:-2]
        made, (sem, out_sem) = (targets if keep else held[len(held) - results :]), refs[-2:]
        copies = []
        for entry, h in zip(() if direct else entries, held):
            copies.append([])
            for i, a in enumerate(entry):
                n = sum(len(c) for c in copies)
                to = h if len(entry) == 1 else h.at[:, pl.ds(a.shape[1] * i, a.shape[1])]
                copies[-1].append(pltpu.make_async_copy(sources[n], to, sem.at[n]))
                copies[-1][-1].start()
        here, leaving = set(range(len(entries)) if direct else ()), []

        def get(i):
            if i not in here:
                here.add(i)
                for copy in copies[i]:
                    copy.wait()
            return sources[i] if direct else held[i]

        def put(i, at=slice(None)):
            if keep:
                return
            copy = pltpu.make_async_copy(made[i].at[at], targets[i].at[at], out_sem.at[len(leaving)])
            copy.start()
            leaving.append(copy)
            whole.discard(i)

        whole = set(range(results))
        body(where_ref, get, put, *made)
        for i in sorted(whole):
            put(i)
        for i in range(len(entries)):
            get(i)
        for copy in leaving:
            copy.wait()

    shapes = [jax.ShapeDtypeStruct(shape, kind) for shape, kind in outs]
    return pl.pallas_call(
        inner,
        out_shape=shapes,
        in_specs=[pl.BlockSpec(memory_space=pltpu.SMEM)]
        + [pl.BlockSpec(memory_space=pltpu.VMEM if direct else pl.ANY)] * count
        + [pl.BlockSpec(memory_space=pl.ANY)] * len(after),
        out_specs=[pl.BlockSpec(memory_space=pltpu.VMEM if keep else pl.ANY)] * results,
        scratch_shapes=[pltpu.VMEM(shape_of(entry), entry[0].dtype) for entry in entries if not direct]
        + [pltpu.VMEM(a.shape, a.dtype) for a in shapes if not keep]
        + [pltpu.SemaphoreType.DMA((count,)), pltpu.SemaphoreType.DMA((most,))],
        compiler_params=pltpu.CompilerParams(vmem_limit_bytes=grant * 1024 * 1024),
        cost_estimate=pl.CostEstimate(flops=flops, bytes_accessed=size, transcendentals=0),
    )(where, *flat, *after)


def use_of(gate, count):
    slots = gate.shape[1]
    lane = lax.broadcasted_iota(jnp.int32, (1, slots), 1)
    use = jnp.where(lane < count, gate, 0.0)
    square = lax.broadcasted_iota(jnp.int32, (slots, slots), 0) == lax.broadcasted_iota(
        jnp.int32, (slots, slots), 1
    )
    return jnp.sum(jnp.where(square, use, 0.0), axis=1, keepdims=True)


def pick_of(token, tok):
    slots = token.shape[1]
    return jnp.where(lax.broadcasted_iota(jnp.int32, (tok, slots), 0) == token, 1.0, 0.0).astype(BF16)


def rows_body(where, get, put, own):
    token, count, gate, tokens = get(2), get(3), get(4), get(0)
    pick = pick_of(token[...], tokens.shape[0])
    own[0] = dot(pick, tokens[...], FIRST).astype(BF16)
    put(0, pl.ds(0, 1))
    own[1] = (use_of(gate[...], count[...]) * dot(pick, get(1)[...], FIRST)).astype(BF16)
    put(0, pl.ds(1, 1))


def turned_body(where, get, put, *turned):
    slots = get(0).shape[1]
    for step in range(N_X):
        for who in range(2):
            for which in range(2):
                turned[step][which, :, slots * who : slots * (who + 1)] = get(who * N_X + step)[which].T
        put(step)


def products_body(where, get, put, part, weights):
    pieces = get(0)
    rows, cols = pieces.shape[1] // 3, pieces.shape[2]
    for i in range(pieces.shape[0]):
        y, z = divmod(i, N_Z)
        place = y // 2 * 8 + z * 2 + y % 2
        for m in range(3):
            weights[place * rows : (place + 1) * rows, cols * m : cols * (m + 1)] = pieces[
                i, rows * m : rows * (m + 1)
            ]
    put(1)
    feat = get(1).shape[2]
    pre, back = 0.0, 0.0
    for step in range(N_X):
        x = get(1 + step)
        at = pl.ds(turn(where, step, feat), feat)
        pre = pre + dot(x[0], weights[at, : 2 * cols])
        back = back + dot(x[1], weights[at, 2 * cols :])
    part[:, : 2 * cols] = pre.astype(BF16)
    part[:, 2 * cols :] = back.astype(BF16)


def terms_body(where, get, put, pieces, acts, send):
    total = get(0)[...].astype(F32) + get(1)[...].astype(F32)
    units = total.shape[1] // 3
    pre_gate, pre_up, grad_hidden = total[:, :units], total[:, units : 2 * units], total[:, 2 * units :]
    sigma = jax.nn.sigmoid(pre_gate)
    acts[:, :units] = (
        grad_hidden * pre_up * sigma * (1.0 + pre_gate * (1.0 - sigma))
    ).astype(BF16)
    acts[:, units : 2 * units] = (grad_hidden * pre_gate * sigma).astype(BF16)
    acts[:, 2 * units :] = (pre_gate * sigma * pre_up).astype(BF16)
    send[...] = acts[send.shape[0] :]
    put(1)
    put(2)
    rows = pieces.shape[1] // 3
    for step in range(N_X):
        turned = get(2 + step)
        both = dot(turned[0], acts[:, : 2 * units]).astype(BF16)
        down = dot(turned[1], acts[:, 2 * units :]).astype(BF16)
        first = turn(where, step, 2 * N_Z)
        for i in range(2 * N_Z):
            y, z = divmod(i, N_Z)
            at = slice((z * 2 + y) * rows, (z * 2 + y + 1) * rows)
            pieces[first + i, :rows] = both[at, :units]
            pieces[first + i, rows : 2 * rows] = both[at, units:]
            pieces[first + i, 2 * rows :] = down[at]
        put(0, pl.ds(first, 2 * N_Z))


def outputs_body(where, get, put, *outs):
    slots, feat = outs[0].shape[1:]
    cols = get(1).shape[1] // 3
    for step in (2, 3, 1, 0):
        at = pl.ds(turn(where, step, feat), feat)
        out, back = 0.0, 0.0
        for who in range(2):
            acts, weights = get(2 * who), get(2 * who + 1)
            out = out + dot(acts[:slots, 2 * cols :], weights[at, 2 * cols :], LAST)
            back = back + dot(acts[:slots, : 2 * cols], weights[at, : 2 * cols], LAST)
        outs[step][0] = out.astype(BF16)
        outs[step][1] = back.astype(BF16)
        put(step)


def tokens_body(where, get, put, mixed, grad_tokens):
    token, count, gate = get(0), get(1), get(2)
    pick, use = pick_of(token[...], mixed.shape[0]), use_of(gate[...], count[...])
    out, back = [sum(get(3 + step)[i].astype(F32) for step in range(N_X)) for i in range(2)]
    mixed[...] = dot(pick, (use * out).astype(BF16)).astype(BF16)
    put(0)
    grad_tokens[...] = dot(pick, back.astype(BF16)).astype(BF16)


def local(tokens, grad_out, slot_token, slot_count, slot_gate, w_gate, w_up, w_down):
    slots, (tok, feat) = slot_token.shape[0], tokens.shape
    rows, cols = w_gate.shape
    token, gate, count = slot_token[None], slot_gate[None], slot_count[None]
    where = (lax.axis_index("narrow") // 2).astype(jnp.int32)[None]
    pick_flops = 4 * slots * tok * feat

    block = jnp.concatenate((w_gate, w_up, w_down), axis=0)
    block = lax.ppermute(block, ("wide", "narrow"), SWAP)
    pieces = jnp.broadcast_to(block[None], (len(OWNERS[0]),) + block.shape)
    pieces = lax.all_to_all(pieces, "wide", 0, 0, axis_index_groups=OWNERS)
    (own,) = call(
        rows_body,
        [((2, slots, feat), BF16)],
        pick_flops,
        where,
        *(tokens, grad_out, token, count, gate),
    )
    near = {step: lax.ppermute(own, "narrow", shift_x(-step)) for step in (1, 3, 2)}
    near = [own] + [near[step] for step in range(1, N_X)]
    core = [lax.ppermute(held, "wide", OTHER_CORE) for held in near]
    turned = call(
        turned_body, [((2, feat, 2 * slots), BF16)] * N_X, pick_flops, where, *near, *core, grant=12, keep=True
    )

    flops = 2 * 3 * 2 * slots * N_X * feat * cols
    part = ((2 * slots, 3 * cols), BF16)
    sent, weights = call(
        products_body,
        [part, ((N_X * feat, 3 * cols), BF16)],
        flops,
        where,
        *(pieces, *([a, b] for a, b in zip(near, core))),
    )
    theirs = lax.ppermute(sent, "narrow", OTHER_HALF)
    terms, acts, send = call(
        terms_body,
        [(pieces.shape, BF16), part, ((slots, 3 * cols), BF16)],
        TERMS,
        where,
        *(sent, theirs, *turned),
        grant=12,
        direct=True,
    )

    core_weights = lax.ppermute(weights, "wide", OTHER_CORE)
    terms, core_weights = lax.optimization_barrier((terms, core_weights))

    terms = lax.all_to_all(terms, "wide", 0, 0, axis_index_groups=OWNERS)
    grads = terms.astype(F32).sum(axis=0).astype(BF16)
    grads = lax.ppermute(grads, ("wide", "narrow"), SWAP_BACK).astype(F32)

    got = lax.ppermute(send, "wide", OTHER_CORE)
    outs = call(
        outputs_body,
        [((2, slots, feat), BF16)] * N_X,
        flops,
        where,
        *(acts, weights, got, core_weights),
    )
    home = {step: lax.ppermute(outs[step], "narrow", shift_x(step)) for step in (1, 3, 2)}
    home = [outs[0]] + [home[step] for step in range(1, N_X)]
    mixed, grad_tokens = call(
        tokens_body,
        [((tok, feat), BF16)] * 2,
        pick_flops,
        where,
        *(token, count, gate, *home),
        grant=12,
        direct=True,
    )
    return mixed, grad_tokens, grads[:rows], grads[rows : 2 * rows], grads[2 * rows :]


def solution(mesh):
    both = P("wide", "narrow")
    in_specs = (both, both, P("wide"), P("wide"), P("wide"), both, both, both)
    return jax.shard_map(
        local, mesh=mesh, in_specs=in_specs, out_specs=(both,) * 5, check_vma=False
    )
```

```python
import jax
import jax.numpy as jnp
from jax import lax
from jax.experimental import pallas as pl
from jax.experimental.pallas import tpu as pltpu
from jax.sharding import PartitionSpec as P

TURN = 2 * 10**10
N_Y, N_Z, N_CORE, N_X = 8, 4, 2, 4
N_WIDE, N_NARROW = N_Y * N_Z * N_CORE, 2 * N_X
F32, BF16 = jnp.float32, jnp.bfloat16
FIRST, LAST, PLAIN = ((0,), (0,)), ((1,), (1,)), ((1,), (0,))


def wide_index(y, z, core):
    return (y * N_Z + z) * N_CORE + core


def swap_pairs():
    pairs = []
    for y in range(N_Y):
        for z in range(N_Z):
            for core in range(N_CORE):
                for n in range(N_NARROW):
                    to = wide_index(y // 2 * 2 + core, z, n % 2)
                    pairs.append((wide_index(y, z, core) * N_NARROW + n, to * N_NARROW + n // 2 * 2 + y % 2))
    return pairs


SWAP = swap_pairs()
SWAP_BACK = [(b, a) for a, b in SWAP]
OTHER_CORE = [(w, w ^ 1) for w in range(N_WIDE)]
OTHER_HALF = [(n, n ^ 1) for n in range(N_NARROW)]
OWNERS = [[wide_index(y, z, core) for y in range(N_Y) for z in range(N_Z)] for core in range(N_CORE)]


def shift_x(by):
    return [(n, (n + 2 * by) % N_NARROW) for n in range(N_NARROW)]


def dot(a, b, dims=PLAIN):
    return lax.dot_general(a, b, (dims, ((), ())), preferred_element_type=F32)


def turn(where, step, size):
    return pl.multiple_of(lax.rem(where[0] + step, N_X) * size, size)


def call(body, outs, flops, where, *args, after=(), grant=60, direct=False, keep=False):
    entries = [a if isinstance(a, list) else [a] for a in args]
    flat = [a for entry in entries for a in entry]
    size = sum(a.size * a.dtype.itemsize for a in flat)
    count, results = len(flat), len(outs)
    most = N_X * results

    def shape_of(entry):
        first, rows, *rest = entry[0].shape if len(entry) > 1 else (0, 0)
        return (first, rows * len(entry), *rest) if len(entry) > 1 else entry[0].shape

    def inner(where_ref, *refs):
        sources, refs = refs[:count], refs[count + len(after) :]
        targets, held = refs[:results], refs[results:-2]
        made, (sem, out_sem) = (targets if keep else held[len(held) - results :]), refs[-2:]
        copies = []
        for entry, h in zip(() if direct else entries, held):
            copies.append([])
            for i, a in enumerate(entry):
                n = sum(len(c) for c in copies)
                to = h if len(entry) == 1 else h.at[:, pl.ds(a.shape[1] * i, a.shape[1])]
                copies[-1].append(pltpu.make_async_copy(sources[n], to, sem.at[n]))
                copies[-1][-1].start()
        here, leaving = set(range(len(entries)) if direct else ()), []

        def get(i):
            if i not in here:
                here.add(i)
                for copy in copies[i]:
                    copy.wait()
            return sources[i] if direct else held[i]

        def put(i, at=slice(None)):
            if keep:
                return
            copy = pltpu.make_async_copy(made[i].at[at], targets[i].at[at], out_sem.at[len(leaving)])
            copy.start()
            leaving.append(copy)
            whole.discard(i)

        whole = set(range(results))
        body(where_ref, get, put, *made)
        for i in sorted(whole):
            put(i)
        for i in range(len(entries)):
            get(i)
        for copy in leaving:
            copy.wait()

    shapes = [jax.ShapeDtypeStruct(shape, kind) for shape, kind in outs]
    return pl.pallas_call(
        inner,
        out_shape=shapes,
        in_specs=[pl.BlockSpec(memory_space=pltpu.SMEM)]
        + [pl.BlockSpec(memory_space=pltpu.VMEM if direct else pl.ANY)] * count
        + [pl.BlockSpec(memory_space=pl.ANY)] * len(after),
        out_specs=[pl.BlockSpec(memory_space=pltpu.VMEM if keep else pl.ANY)] * results,
        scratch_shapes=[pltpu.VMEM(shape_of(entry), entry[0].dtype) for entry in entries if not direct]
        + [pltpu.VMEM(a.shape, a.dtype) for a in shapes if not keep]
        + [pltpu.SemaphoreType.DMA((count,)), pltpu.SemaphoreType.DMA((most,))],
        compiler_params=pltpu.CompilerParams(vmem_limit_bytes=grant * 1024 * 1024),
        cost_estimate=pl.CostEstimate(flops=flops, bytes_accessed=size, transcendentals=0),
    )(where, *flat, *after)


def use_of(gate, count):
    slots = gate.shape[1]
    lane = lax.broadcasted_iota(jnp.int32, (1, slots), 1)
    use = jnp.where(lane < count, gate, 0.0)
    square = lax.broadcasted_iota(jnp.int32, (slots, slots), 0) == lax.broadcasted_iota(
        jnp.int32, (slots, slots), 1
    )
    return jnp.sum(jnp.where(square, use, 0.0), axis=1, keepdims=True)


def pick_of(token, tok):
    slots = token.shape[1]
    return jnp.where(lax.broadcasted_iota(jnp.int32, (tok, slots), 0) == token, 1.0, 0.0).astype(BF16)


def rows_body(where, get, put, own):
    token, count, gate, tokens = get(2), get(3), get(4), get(0)
    pick = pick_of(token[...], tokens.shape[0])
    own[0] = dot(pick, tokens[...], FIRST).astype(BF16)
    put(0, pl.ds(0, 1))
    own[1] = (use_of(gate[...], count[...]) * dot(pick, get(1)[...], FIRST)).astype(BF16)
    put(0, pl.ds(1, 1))


def turned_body(where, get, put, *turned):
    slots = get(0).shape[1]
    for step in range(N_X):
        for who in range(2):
            for which in range(2):
                turned[step][which, :, slots * who : slots * (who + 1)] = get(who * N_X + step)[which].T
        put(step)


def products_body(where, get, put, part, weights):
    pieces = get(0)
    rows, cols = pieces.shape[1] // 3, pieces.shape[2]
    for i in range(pieces.shape[0]):
        y, z = divmod(i, N_Z)
        place = y // 2 * 8 + z * 2 + y % 2
        for m in range(3):
            weights[place * rows : (place + 1) * rows, cols * m : cols * (m + 1)] = pieces[
                i, rows * m : rows * (m + 1)
            ]
    put(1)
    feat = get(1).shape[2]
    pre, back = 0.0, 0.0
    for step in range(N_X):
        x = get(1 + step)
        at = pl.ds(turn(where, step, feat), feat)
        pre = pre + dot(x[0], weights[at, : 2 * cols])
        back = back + dot(x[1], weights[at, 2 * cols :])
    part[:, : 2 * cols] = pre.astype(BF16)
    part[:, 2 * cols :] = back.astype(BF16)


def terms_body(where, get, put, pieces, acts, send):
    total = get(0)[...].astype(F32) + get(1)[...].astype(F32)
    units = total.shape[1] // 3
    pre_gate, pre_up, grad_hidden = total[:, :units], total[:, units : 2 * units], total[:, 2 * units :]
    sigma = jax.nn.sigmoid(pre_gate)
    acts[:, :units] = (
        grad_hidden * pre_up * sigma * (1.0 + pre_gate * (1.0 - sigma))
    ).astype(BF16)
    acts[:, units : 2 * units] = (grad_hidden * pre_gate * sigma).astype(BF16)
    acts[:, 2 * units :] = (pre_gate * sigma * pre_up).astype(BF16)
    send[...] = acts[send.shape[0] :]
    put(1)
    put(2)
    rows = pieces.shape[1] // 3
    for step in range(N_X):
        turned = get(2 + step)
        both = dot(turned[0], acts[:, : 2 * units]).astype(BF16)
        down = dot(turned[1], acts[:, 2 * units :]).astype(BF16)
        first = turn(where, step, 2 * N_Z)
        for i in range(2 * N_Z):
            y, z = divmod(i, N_Z)
            at = slice((z * 2 + y) * rows, (z * 2 + y + 1) * rows)
            pieces[first + i, :rows] = both[at, :units]
            pieces[first + i, rows : 2 * rows] = both[at, units:]
            pieces[first + i, 2 * rows :] = down[at]
        put(0, pl.ds(first, 2 * N_Z))


def outputs_body(where, get, put, *outs):
    slots, feat = outs[0].shape[1:]
    cols = get(1).shape[1] // 3
    for step in (2, 3, 1, 0):
        at = pl.ds(turn(where, step, feat), feat)
        out, back = 0.0, 0.0
        for who in range(2):
            acts, weights = get(2 * who), get(2 * who + 1)
            out = out + dot(acts[:slots, 2 * cols :], weights[at, 2 * cols :], LAST)
            back = back + dot(acts[:slots, : 2 * cols], weights[at, : 2 * cols], LAST)
        outs[step][0] = out.astype(BF16)
        outs[step][1] = back.astype(BF16)
        put(step)


def tokens_body(where, get, put, mixed, grad_tokens):
    token, count, gate = get(0), get(1), get(2)
    pick, use = pick_of(token[...], mixed.shape[0]), use_of(gate[...], count[...])
    out, back = [sum(get(3 + step)[i].astype(F32) for step in range(N_X)) for i in range(2)]
    mixed[...] = dot(pick, (use * out).astype(BF16)).astype(BF16)
    put(0)
    grad_tokens[...] = dot(pick, back.astype(BF16)).astype(BF16)


def local(tokens, grad_out, slot_token, slot_count, slot_gate, w_gate, w_up, w_down):
    slots, (tok, feat) = slot_token.shape[0], tokens.shape
    rows, cols = w_gate.shape
    token, gate, count = slot_token[None], slot_gate[None], slot_count[None]
    where = (lax.axis_index("narrow") // 2).astype(jnp.int32)[None]
    pick_flops = 4 * slots * tok * feat

    block = jnp.concatenate((w_gate, w_up, w_down), axis=0)
    block = lax.ppermute(block, ("wide", "narrow"), SWAP)
    pieces = jnp.broadcast_to(block[None], (len(OWNERS[0]),) + block.shape)
    pieces = lax.all_to_all(pieces, "wide", 0, 0, axis_index_groups=OWNERS)
    (own,) = call(
        rows_body,
        [((2, slots, feat), BF16)],
        pick_flops,
        where,
        *(tokens, grad_out, token, count, gate),
    )
    near = {step: lax.ppermute(own, "narrow", shift_x(-step)) for step in (1, 3, 2)}
    near = [own] + [near[step] for step in range(1, N_X)]
    core = [lax.ppermute(held, "wide", OTHER_CORE) for held in near]
    turned = call(
        turned_body, [((2, feat, 2 * slots), BF16)] * N_X, TURN, where, *near, *core, grant=12, keep=True
    )

    flops = 2 * 3 * 2 * slots * N_X * feat * cols
    part = ((2 * slots, 3 * cols), BF16)
    sent, weights = call(
        products_body,
        [part, ((N_X * feat, 3 * cols), BF16)],
        flops,
        where,
        *(pieces, *([a, b] for a, b in zip(near, core))),
    )
    theirs = lax.ppermute(sent, "narrow", OTHER_HALF)
    core_weights = lax.ppermute(weights, "wide", OTHER_CORE)
    theirs, core_weights = lax.optimization_barrier((theirs, core_weights))
    terms, acts, send = call(
        terms_body,
        [(pieces.shape, BF16), part, ((slots, 3 * cols), BF16)],
        flops,
        where,
        *(sent, theirs, *turned),
        grant=12,
        direct=True,
    )


    terms = lax.all_to_all(terms, "wide", 0, 0, axis_index_groups=OWNERS)
    grads = terms.astype(F32).sum(axis=0).astype(BF16)
    grads = lax.ppermute(grads, ("wide", "narrow"), SWAP_BACK).astype(F32)

    got = lax.ppermute(send, "wide", OTHER_CORE)
    outs = call(
        outputs_body,
        [((2, slots, feat), BF16)] * N_X,
        flops,
        where,
        *(acts, weights, got, core_weights),
    )
    home = {step: lax.ppermute(outs[step], "narrow", shift_x(step)) for step in (1, 3, 2)}
    home = [outs[0]] + [home[step] for step in range(1, N_X)]
    mixed, grad_tokens = call(
        tokens_body,
        [((tok, feat), BF16)] * 2,
        pick_flops,
        where,
        *(token, count, gate, *home),
    )
    return mixed, grad_tokens, grads[:rows], grads[rows : 2 * rows], grads[2 * rows :]


def solution(mesh):
    both = P("wide", "narrow")
    in_specs = (both, both, P("wide"), P("wide"), P("wide"), both, both, both)
    return jax.shard_map(
        local, mesh=mesh, in_specs=in_specs, out_specs=(both,) * 5, check_vma=False
    )
```

```python
import jax
import jax.numpy as jnp
from jax import lax
from jax.experimental import pallas as pl
from jax.experimental.pallas import tpu as pltpu
from jax.sharding import PartitionSpec as P

TURN = 2 * 10**10
N_Y, N_Z, N_CORE, N_X = 8, 4, 2, 4
N_WIDE, N_NARROW = N_Y * N_Z * N_CORE, 2 * N_X
F32, BF16 = jnp.float32, jnp.bfloat16
FIRST, LAST, PLAIN = ((0,), (0,)), ((1,), (1,)), ((1,), (0,))


def wide_index(y, z, core):
    return (y * N_Z + z) * N_CORE + core


def swap_pairs():
    pairs = []
    for y in range(N_Y):
        for z in range(N_Z):
            for core in range(N_CORE):
                for n in range(N_NARROW):
                    to = wide_index(y // 2 * 2 + core, z, n % 2)
                    pairs.append((wide_index(y, z, core) * N_NARROW + n, to * N_NARROW + n // 2 * 2 + y % 2))
    return pairs


SWAP = swap_pairs()
SWAP_BACK = [(b, a) for a, b in SWAP]
OTHER_CORE = [(w, w ^ 1) for w in range(N_WIDE)]
OTHER_HALF = [(n, n ^ 1) for n in range(N_NARROW)]
OWNERS = [[wide_index(y, z, core) for y in range(N_Y) for z in range(N_Z)] for core in range(N_CORE)]


def shift_x(by):
    return [(n, (n + 2 * by) % N_NARROW) for n in range(N_NARROW)]


def dot(a, b, dims=PLAIN):
    return lax.dot_general(a, b, (dims, ((), ())), preferred_element_type=F32)


def turn(where, step, size):
    return pl.multiple_of(lax.rem(where[0] + step, N_X) * size, size)


def call(body, outs, flops, where, *args, after=(), grant=60, direct=False, keep=False):
    entries = [a if isinstance(a, list) else [a] for a in args]
    flat = [a for entry in entries for a in entry]
    size = sum(a.size * a.dtype.itemsize for a in flat)
    count, results = len(flat), len(outs)
    most = N_X * results

    def shape_of(entry):
        first, rows, *rest = entry[0].shape if len(entry) > 1 else (0, 0)
        return (first, rows * len(entry), *rest) if len(entry) > 1 else entry[0].shape

    def inner(where_ref, *refs):
        sources, refs = refs[:count], refs[count + len(after) :]
        targets, held = refs[:results], refs[results:-2]
        made, (sem, out_sem) = (targets if keep else held[len(held) - results :]), refs[-2:]
        copies = []
        for entry, h in zip(() if direct else entries, held):
            copies.append([])
            for i, a in enumerate(entry):
                n = sum(len(c) for c in copies)
                to = h if len(entry) == 1 else h.at[:, pl.ds(a.shape[1] * i, a.shape[1])]
                copies[-1].append(pltpu.make_async_copy(sources[n], to, sem.at[n]))
                copies[-1][-1].start()
        here, leaving = set(range(len(entries)) if direct else ()), []

        def get(i):
            if i not in here:
                here.add(i)
                for copy in copies[i]:
                    copy.wait()
            return sources[i] if direct else held[i]

        def put(i, at=slice(None)):
            if keep:
                return
            copy = pltpu.make_async_copy(made[i].at[at], targets[i].at[at], out_sem.at[len(leaving)])
            copy.start()
            leaving.append(copy)
            whole.discard(i)

        whole = set(range(results))
        body(where_ref, get, put, *made)
        for i in sorted(whole):
            put(i)
        for i in range(len(entries)):
            get(i)
        for copy in leaving:
            copy.wait()

    shapes = [jax.ShapeDtypeStruct(shape, kind) for shape, kind in outs]
    return pl.pallas_call(
        inner,
        out_shape=shapes,
        in_specs=[pl.BlockSpec(memory_space=pltpu.SMEM)]
        + [pl.BlockSpec(memory_space=pltpu.VMEM if direct else pl.ANY)] * count
        + [pl.BlockSpec(memory_space=pl.ANY)] * len(after),
        out_specs=[pl.BlockSpec(memory_space=pltpu.VMEM if keep else pl.ANY)] * results,
        scratch_shapes=[pltpu.VMEM(shape_of(entry), entry[0].dtype) for entry in entries if not direct]
        + [pltpu.VMEM(a.shape, a.dtype) for a in shapes if not keep]
        + [pltpu.SemaphoreType.DMA((count,)), pltpu.SemaphoreType.DMA((most,))],
        compiler_params=pltpu.CompilerParams(vmem_limit_bytes=grant * 1024 * 1024),
        cost_estimate=pl.CostEstimate(flops=flops, bytes_accessed=size, transcendentals=0),
    )(where, *flat, *after)


def use_of(gate, count):
    slots = gate.shape[1]
    lane = lax.broadcasted_iota(jnp.int32, (1, slots), 1)
    use = jnp.where(lane < count, gate, 0.0)
    square = lax.broadcasted_iota(jnp.int32, (slots, slots), 0) == lax.broadcasted_iota(
        jnp.int32, (slots, slots), 1
    )
    return jnp.sum(jnp.where(square, use, 0.0), axis=1, keepdims=True)


def pick_of(token, tok):
    slots = token.shape[1]
    return jnp.where(lax.broadcasted_iota(jnp.int32, (tok, slots), 0) == token, 1.0, 0.0).astype(BF16)


def rows_body(where, get, put, own):
    token, count, gate, tokens = get(2), get(3), get(4), get(0)
    pick = pick_of(token[...], tokens.shape[0])
    own[0] = dot(pick, tokens[...], FIRST).astype(BF16)
    put(0, pl.ds(0, 1))
    own[1] = (use_of(gate[...], count[...]) * dot(pick, get(1)[...], FIRST)).astype(BF16)
    put(0, pl.ds(1, 1))


def turned_body(where, get, put, *turned):
    slots = get(0).shape[1]
    for step in range(N_X):
        for who in range(2):
            for which in range(2):
                turned[step][which, :, slots * who : slots * (who + 1)] = get(who * N_X + step)[which].T
        put(step)


def products_body(where, get, put, part, weights):
    pieces = get(0)
    rows, cols = pieces.shape[1] // 3, pieces.shape[2]
    for i in range(pieces.shape[0]):
        y, z = divmod(i, N_Z)
        place = y // 2 * 8 + z * 2 + y % 2
        for m in range(3):
            weights[place * rows : (place + 1) * rows, cols * m : cols * (m + 1)] = pieces[
                i, rows * m : rows * (m + 1)
            ]
    put(1)
    feat = get(1).shape[2]
    pre, back = 0.0, 0.0
    for step in range(N_X):
        x = get(1 + step)
        at = pl.ds(turn(where, step, feat), feat)
        pre = pre + dot(x[0], weights[at, : 2 * cols])
        back = back + dot(x[1], weights[at, 2 * cols :])
    part[:, : 2 * cols] = pre.astype(BF16)
    part[:, 2 * cols :] = back.astype(BF16)


def terms_body(where, get, put, pieces, acts, send):
    total = get(0)[...].astype(F32) + get(1)[...].astype(F32)
    units = total.shape[1] // 3
    pre_gate, pre_up, grad_hidden = total[:, :units], total[:, units : 2 * units], total[:, 2 * units :]
    sigma = jax.nn.sigmoid(pre_gate)
    acts[:, :units] = (
        grad_hidden * pre_up * sigma * (1.0 + pre_gate * (1.0 - sigma))
    ).astype(BF16)
    acts[:, units : 2 * units] = (grad_hidden * pre_gate * sigma).astype(BF16)
    acts[:, 2 * units :] = (pre_gate * sigma * pre_up).astype(BF16)
    send[...] = acts[send.shape[0] :]
    put(1)
    put(2)
    rows = pieces.shape[1] // 3
    for step in range(N_X):
        turned = get(2 + step)
        both = dot(turned[0], acts[:, : 2 * units]).astype(BF16)
        down = dot(turned[1], acts[:, 2 * units :]).astype(BF16)
        first = turn(where, step, 2 * N_Z)
        for i in range(2 * N_Z):
            y, z = divmod(i, N_Z)
            at = slice((z * 2 + y) * rows, (z * 2 + y + 1) * rows)
            pieces[first + i, :rows] = both[at, :units]
            pieces[first + i, rows : 2 * rows] = both[at, units:]
            pieces[first + i, 2 * rows :] = down[at]
        put(0, pl.ds(first, 2 * N_Z))


def outputs_body(where, get, put, *outs):
    slots, feat = outs[0].shape[1:]
    cols = get(1).shape[1] // 3
    for step in (2, 3, 1, 0):
        at = pl.ds(turn(where, step, feat), feat)
        out, back = 0.0, 0.0
        for who in range(2):
            acts, weights = get(2 * who), get(2 * who + 1)
            out = out + dot(acts[:slots, 2 * cols :], weights[at, 2 * cols :], LAST)
            back = back + dot(acts[:slots, : 2 * cols], weights[at, : 2 * cols], LAST)
        outs[step][0] = out.astype(BF16)
        outs[step][1] = back.astype(BF16)
        put(step)


def tokens_body(where, get, put, mixed, grad_tokens):
    token, count, gate = get(0), get(1), get(2)
    pick, use = pick_of(token[...], mixed.shape[0]), use_of(gate[...], count[...])
    out, back = [sum(get(3 + step)[i].astype(F32) for step in range(N_X)) for i in range(2)]
    mixed[...] = dot(pick, (use * out).astype(BF16)).astype(BF16)
    put(0)
    grad_tokens[...] = dot(pick, back.astype(BF16)).astype(BF16)


def local(tokens, grad_out, slot_token, slot_count, slot_gate, w_gate, w_up, w_down):
    slots, (tok, feat) = slot_token.shape[0], tokens.shape
    rows, cols = w_gate.shape
    token, gate, count = slot_token[None], slot_gate[None], slot_count[None]
    where = (lax.axis_index("narrow") // 2).astype(jnp.int32)[None]
    pick_flops = 4 * slots * tok * feat

    block = jnp.concatenate((w_gate, w_up, w_down), axis=0)
    block = lax.ppermute(block, ("wide", "narrow"), SWAP)
    (own,) = call(
        rows_body,
        [((2, slots, feat), BF16)],
        pick_flops,
        where,
        *(tokens, grad_out, token, count, gate),
    )
    block, own = lax.optimization_barrier((block, own))
    pieces = jnp.broadcast_to(block[None], (len(OWNERS[0]),) + block.shape)
    pieces = lax.all_to_all(pieces, "wide", 0, 0, axis_index_groups=OWNERS)
    near = {step: lax.ppermute(own, "narrow", shift_x(-step)) for step in (1, 3, 2)}
    near = [own] + [near[step] for step in range(1, N_X)]
    core = [lax.ppermute(held, "wide", OTHER_CORE) for held in near]
    turned = call(
        turned_body, [((2, feat, 2 * slots), BF16)] * N_X, TURN, where, *near, *core, grant=12, keep=True
    )

    flops = 2 * 3 * 2 * slots * N_X * feat * cols
    part = ((2 * slots, 3 * cols), BF16)
    sent, weights = call(
        products_body,
        [part, ((N_X * feat, 3 * cols), BF16)],
        flops,
        where,
        *(pieces, *([a, b] for a, b in zip(near, core))),
    )
    theirs = lax.ppermute(sent, "narrow", OTHER_HALF)
    core_weights = lax.ppermute(weights, "wide", OTHER_CORE)
    theirs, core_weights = lax.optimization_barrier((theirs, core_weights))
    terms, acts, send = call(
        terms_body,
        [(pieces.shape, BF16), part, ((slots, 3 * cols), BF16)],
        flops,
        where,
        *(sent, theirs, *turned),
        grant=12,
        direct=True,
    )


    terms = lax.all_to_all(terms, "wide", 0, 0, axis_index_groups=OWNERS)
    grads = terms.astype(F32).sum(axis=0).astype(BF16)
    grads = lax.ppermute(grads, ("wide", "narrow"), SWAP_BACK).astype(F32)

    got = lax.ppermute(send, "wide", OTHER_CORE)
    outs = call(
        outputs_body,
        [((2, slots, feat), BF16)] * N_X,
        flops,
        where,
        *(acts, weights, got, core_weights),
    )
    home = {step: lax.ppermute(outs[step], "narrow", shift_x(step)) for step in (1, 3, 2)}
    home = [outs[0]] + [home[step] for step in range(1, N_X)]
    mixed, grad_tokens = call(
        tokens_body,
        [((tok, feat), BF16)] * 2,
        pick_flops,
        where,
        *(token, count, gate, *home),
    )
    return mixed, grad_tokens, grads[:rows], grads[rows : 2 * rows], grads[2 * rows :]


def solution(mesh):
    both = P("wide", "narrow")
    in_specs = (both, both, P("wide"), P("wide"), P("wide"), both, both, both)
    return jax.shard_map(
        local, mesh=mesh, in_specs=in_specs, out_specs=(both,) * 5, check_vma=False
    )
```

```python
import jax
import jax.numpy as jnp
from jax import lax
from jax.experimental import pallas as pl
from jax.experimental.pallas import tpu as pltpu
from jax.sharding import PartitionSpec as P

TURN = 2 * 10**10
N_Y, N_Z, N_CORE, N_X = 8, 4, 2, 4
N_WIDE, N_NARROW = N_Y * N_Z * N_CORE, 2 * N_X
F32, BF16 = jnp.float32, jnp.bfloat16
FIRST, LAST, PLAIN = ((0,), (0,)), ((1,), (1,)), ((1,), (0,))


def wide_index(y, z, core):
    return (y * N_Z + z) * N_CORE + core


def swap_pairs():
    pairs = []
    for y in range(N_Y):
        for z in range(N_Z):
            for core in range(N_CORE):
                for n in range(N_NARROW):
                    to = wide_index(y // 2 * 2 + core, z, n % 2)
                    pairs.append((wide_index(y, z, core) * N_NARROW + n, to * N_NARROW + n // 2 * 2 + y % 2))
    return pairs


SWAP = swap_pairs()
SWAP_BACK = [(b, a) for a, b in SWAP]
OTHER_CORE = [(w, w ^ 1) for w in range(N_WIDE)]
OTHER_HALF = [(n, n ^ 1) for n in range(N_NARROW)]
OWNERS = [[wide_index(y, z, core) for y in range(N_Y) for z in range(N_Z)] for core in range(N_CORE)]


def shift_x(by):
    return [(n, (n + 2 * by) % N_NARROW) for n in range(N_NARROW)]


def dot(a, b, dims=PLAIN):
    return lax.dot_general(a, b, (dims, ((), ())), preferred_element_type=F32)


def turn(where, step, size):
    return pl.multiple_of(lax.rem(where[0] + step, N_X) * size, size)


def call(body, outs, flops, where, *args, after=(), grant=60, direct=False, keep=False):
    entries = [a if isinstance(a, list) else [a] for a in args]
    flat = [a for entry in entries for a in entry]
    size = sum(a.size * a.dtype.itemsize for a in flat)
    count, results = len(flat), len(outs)
    most = N_X * results

    def shape_of(entry):
        first, rows, *rest = entry[0].shape if len(entry) > 1 else (0, 0)
        return (first, rows * len(entry), *rest) if len(entry) > 1 else entry[0].shape

    def inner(where_ref, *refs):
        sources, refs = refs[:count], refs[count + len(after) :]
        targets, held = refs[:results], refs[results:-2]
        made, (sem, out_sem) = (targets if keep else held[len(held) - results :]), refs[-2:]
        copies = []
        for entry, h in zip(() if direct else entries, held):
            copies.append([])
            for i, a in enumerate(entry):
                n = sum(len(c) for c in copies)
                to = h if len(entry) == 1 else h.at[:, pl.ds(a.shape[1] * i, a.shape[1])]
                copies[-1].append(pltpu.make_async_copy(sources[n], to, sem.at[n]))
                copies[-1][-1].start()
        here, leaving = set(range(len(entries)) if direct else ()), []

        def get(i):
            if i not in here:
                here.add(i)
                for copy in copies[i]:
                    copy.wait()
            return sources[i] if direct else held[i]

        def put(i, at=slice(None)):
            if keep:
                return
            copy = pltpu.make_async_copy(made[i].at[at], targets[i].at[at], out_sem.at[len(leaving)])
            copy.start()
            leaving.append(copy)
            whole.discard(i)

        whole = set(range(results))
        body(where_ref, get, put, *made)
        for i in sorted(whole):
            put(i)
        for i in range(len(entries)):
            get(i)
        for copy in leaving:
            copy.wait()

    shapes = [jax.ShapeDtypeStruct(shape, kind) for shape, kind in outs]
    return pl.pallas_call(
        inner,
        out_shape=shapes,
        in_specs=[pl.BlockSpec(memory_space=pltpu.SMEM)]
        + [pl.BlockSpec(memory_space=pltpu.VMEM if direct else pl.ANY)] * count
        + [pl.BlockSpec(memory_space=pl.ANY)] * len(after),
        out_specs=[pl.BlockSpec(memory_space=pltpu.VMEM if keep else pl.ANY)] * results,
        scratch_shapes=[pltpu.VMEM(shape_of(entry), entry[0].dtype) for entry in entries if not direct]
        + [pltpu.VMEM(a.shape, a.dtype) for a in shapes if not keep]
        + [pltpu.SemaphoreType.DMA((count,)), pltpu.SemaphoreType.DMA((most,))],
        compiler_params=pltpu.CompilerParams(vmem_limit_bytes=grant * 1024 * 1024),
        cost_estimate=pl.CostEstimate(flops=flops, bytes_accessed=size, transcendentals=0),
    )(where, *flat, *after)


def use_of(gate, count):
    slots = gate.shape[1]
    lane = lax.broadcasted_iota(jnp.int32, (1, slots), 1)
    use = jnp.where(lane < count, gate, 0.0)
    square = lax.broadcasted_iota(jnp.int32, (slots, slots), 0) == lax.broadcasted_iota(
        jnp.int32, (slots, slots), 1
    )
    return jnp.sum(jnp.where(square, use, 0.0), axis=1, keepdims=True)


def pick_of(token, tok):
    slots = token.shape[1]
    return jnp.where(lax.broadcasted_iota(jnp.int32, (tok, slots), 0) == token, 1.0, 0.0).astype(BF16)


def rows_body(where, get, put, own):
    token, count, gate, tokens = get(2), get(3), get(4), get(0)
    pick = pick_of(token[...], tokens.shape[0])
    own[0] = dot(pick, tokens[...], FIRST).astype(BF16)
    put(0, pl.ds(0, 1))
    own[1] = (use_of(gate[...], count[...]) * dot(pick, get(1)[...], FIRST)).astype(BF16)
    put(0, pl.ds(1, 1))


def turned_body(where, get, put, *turned):
    slots = get(0).shape[1]
    for step in range(N_X):
        for who in range(2):
            for which in range(2):
                turned[step][which, :, slots * who : slots * (who + 1)] = get(who * N_X + step)[which].T
        put(step)


def products_body(where, get, put, part, weights):
    pieces = get(0)
    rows, cols = pieces.shape[1] // 3, pieces.shape[2]
    for i in range(pieces.shape[0]):
        y, z = divmod(i, N_Z)
        place = y // 2 * 8 + z * 2 + y % 2
        for m in range(3):
            weights[place * rows : (place + 1) * rows, cols * m : cols * (m + 1)] = pieces[
                i, rows * m : rows * (m + 1)
            ]
    put(1)
    feat = get(1).shape[2]
    pre, back = 0.0, 0.0
    for step in range(N_X):
        x = get(1 + step)
        at = pl.ds(turn(where, step, feat), feat)
        pre = pre + dot(x[0], weights[at, : 2 * cols])
        back = back + dot(x[1], weights[at, 2 * cols :])
    part[:, : 2 * cols] = pre.astype(BF16)
    part[:, 2 * cols :] = back.astype(BF16)


def acts_body(where, get, put, acts, send):
    total = get(0)[...].astype(F32) + get(1)[...].astype(F32)
    units = total.shape[1] // 3
    pre_gate, pre_up, grad_hidden = total[:, :units], total[:, units : 2 * units], total[:, 2 * units :]
    sigma = jax.nn.sigmoid(pre_gate)
    acts[:, :units] = (
        grad_hidden * pre_up * sigma * (1.0 + pre_gate * (1.0 - sigma))
    ).astype(BF16)
    acts[:, units : 2 * units] = (grad_hidden * pre_gate * sigma).astype(BF16)
    acts[:, 2 * units :] = (pre_gate * sigma * pre_up).astype(BF16)
    send[...] = acts[send.shape[0] :]


def terms_body(where, get, put, pieces):
    acts = get(0)
    rows, units = pieces.shape[1] // 3, pieces.shape[2]
    for step in range(N_X):
        turned = get(1 + step)
        both = dot(turned[0], acts[:, : 2 * units]).astype(BF16)
        down = dot(turned[1], acts[:, 2 * units :]).astype(BF16)
        first = turn(where, step, 2 * N_Z)
        for i in range(2 * N_Z):
            y, z = divmod(i, N_Z)
            at = slice((z * 2 + y) * rows, (z * 2 + y + 1) * rows)
            pieces[first + i, :rows] = both[at, :units]
            pieces[first + i, rows : 2 * rows] = both[at, units:]
            pieces[first + i, 2 * rows :] = down[at]
        put(0, pl.ds(first, 2 * N_Z))


def outputs_body(where, get, put, *outs):
    slots, feat = outs[0].shape[1:]
    cols = get(1).shape[1] // 3
    for step in (2, 3, 1, 0):
        at = pl.ds(turn(where, step, feat), feat)
        out, back = 0.0, 0.0
        for who in range(2):
            acts, weights = get(2 * who), get(2 * who + 1)
            out = out + dot(acts[:slots, 2 * cols :], weights[at, 2 * cols :], LAST)
            back = back + dot(acts[:slots, : 2 * cols], weights[at, : 2 * cols], LAST)
        outs[step][0] = out.astype(BF16)
        outs[step][1] = back.astype(BF16)
        put(step)


def tokens_body(where, get, put, mixed, grad_tokens):
    token, count, gate = get(0), get(1), get(2)
    pick, use = pick_of(token[...], mixed.shape[0]), use_of(gate[...], count[...])
    out, back = [sum(get(3 + step)[i].astype(F32) for step in range(N_X)) for i in range(2)]
    mixed[...] = dot(pick, (use * out).astype(BF16)).astype(BF16)
    put(0)
    grad_tokens[...] = dot(pick, back.astype(BF16)).astype(BF16)


def local(tokens, grad_out, slot_token, slot_count, slot_gate, w_gate, w_up, w_down):
    slots, (tok, feat) = slot_token.shape[0], tokens.shape
    rows, cols = w_gate.shape
    token, gate, count = slot_token[None], slot_gate[None], slot_count[None]
    where = (lax.axis_index("narrow") // 2).astype(jnp.int32)[None]
    pick_flops = 4 * slots * tok * feat

    block = jnp.concatenate((w_gate, w_up, w_down), axis=0)
    block = lax.ppermute(block, ("wide", "narrow"), SWAP)
    (own,) = call(
        rows_body,
        [((2, slots, feat), BF16)],
        pick_flops,
        where,
        *(tokens, grad_out, token, count, gate),
    )
    block, own = lax.optimization_barrier((block, own))
    pieces = jnp.broadcast_to(block[None], (len(OWNERS[0]),) + block.shape)
    pieces = lax.all_to_all(pieces, "wide", 0, 0, axis_index_groups=OWNERS)
    near = {step: lax.ppermute(own, "narrow", shift_x(-step)) for step in (1, 3, 2)}
    near = [own] + [near[step] for step in range(1, N_X)]
    core = [lax.ppermute(held, "wide", OTHER_CORE) for held in near]
    turned = call(
        turned_body, [((2, feat, 2 * slots), BF16)] * N_X, TURN, where, *near, *core, grant=12, keep=True
    )

    flops = 2 * 3 * 2 * slots * N_X * feat * cols
    part = ((2 * slots, 3 * cols), BF16)
    sent, weights = call(
        products_body,
        [part, ((N_X * feat, 3 * cols), BF16)],
        flops,
        where,
        *(pieces, *([a, b] for a, b in zip(near, core))),
    )
    theirs = lax.ppermute(sent, "narrow", OTHER_HALF)
    core_weights = lax.ppermute(weights, "wide", OTHER_CORE)
    theirs, core_weights = lax.optimization_barrier((theirs, core_weights))
    acts, send = call(
        acts_body,
        [part, ((slots, 3 * cols), BF16)],
        20 * 2 * slots * 3 * cols,
        where,
        *(sent, theirs),
        grant=12,
        direct=True,
        keep=True,
    )
    (terms,) = call(
        terms_body, [(pieces.shape, BF16)], flops, where, acts, *turned, grant=12, direct=True
    )

    terms = lax.all_to_all(terms, "wide", 0, 0, axis_index_groups=OWNERS)
    grads = terms.astype(F32).sum(axis=0).astype(BF16)
    grads = lax.ppermute(grads, ("wide", "narrow"), SWAP_BACK).astype(F32)

    got = lax.ppermute(send, "wide", OTHER_CORE)
    outs = call(
        outputs_body,
        [((2, slots, feat), BF16)] * N_X,
        flops,
        where,
        *(acts, weights, got, core_weights),
    )
    home = {step: lax.ppermute(outs[step], "narrow", shift_x(step)) for step in (1, 3, 2)}
    home = [outs[0]] + [home[step] for step in range(1, N_X)]
    mixed, grad_tokens = call(
        tokens_body,
        [((tok, feat), BF16)] * 2,
        pick_flops,
        where,
        *(token, count, gate, *home),
    )
    return mixed, grad_tokens, grads[:rows], grads[rows : 2 * rows], grads[2 * rows :]


def solution(mesh):
    both = P("wide", "narrow")
    in_specs = (both, both, P("wide"), P("wide"), P("wide"), both, both, both)
    return jax.shard_map(
        local, mesh=mesh, in_specs=in_specs, out_specs=(both,) * 5, check_vma=False
    )
```

```python
import jax
import jax.numpy as jnp
from jax import lax
from jax.experimental import pallas as pl
from jax.experimental.pallas import tpu as pltpu
from jax.sharding import PartitionSpec as P

TURN = 2 * 10**10
N_Y, N_Z, N_CORE, N_X = 8, 4, 2, 4
N_WIDE, N_NARROW = N_Y * N_Z * N_CORE, 2 * N_X
F32, BF16 = jnp.float32, jnp.bfloat16
FIRST, LAST, PLAIN = ((0,), (0,)), ((1,), (1,)), ((1,), (0,))


def wide_index(y, z, core):
    return (y * N_Z + z) * N_CORE + core


def swap_pairs():
    pairs = []
    for y in range(N_Y):
        for z in range(N_Z):
            for core in range(N_CORE):
                for n in range(N_NARROW):
                    to = wide_index(y // 2 * 2 + core, z, n % 2)
                    pairs.append((wide_index(y, z, core) * N_NARROW + n, to * N_NARROW + n // 2 * 2 + y % 2))
    return pairs


SWAP = swap_pairs()
SWAP_BACK = [(b, a) for a, b in SWAP]
OTHER_CORE = [(w, w ^ 1) for w in range(N_WIDE)]
OTHER_HALF = [(n, n ^ 1) for n in range(N_NARROW)]
OWNERS = [[wide_index(y, z, core) for y in range(N_Y) for z in range(N_Z)] for core in range(N_CORE)]


def shift_x(by):
    return [(n, (n + 2 * by) % N_NARROW) for n in range(N_NARROW)]


def dot(a, b, dims=PLAIN):
    return lax.dot_general(a, b, (dims, ((), ())), preferred_element_type=F32)


def turn(where, step, size):
    return pl.multiple_of(lax.rem(where[0] + step, N_X) * size, size)


def call(body, outs, flops, where, *args, after=(), grant=60, direct=False, keep=False):
    entries = [a if isinstance(a, list) else [a] for a in args]
    flat = [a for entry in entries for a in entry]
    size = sum(a.size * a.dtype.itemsize for a in flat)
    count, results = len(flat), len(outs)
    most = N_X * results

    def shape_of(entry):
        first, rows, *rest = entry[0].shape if len(entry) > 1 else (0, 0)
        return (first, rows * len(entry), *rest) if len(entry) > 1 else entry[0].shape

    def inner(where_ref, *refs):
        sources, refs = refs[:count], refs[count + len(after) :]
        targets, held = refs[:results], refs[results:-2]
        made, (sem, out_sem) = (targets if keep else held[len(held) - results :]), refs[-2:]
        copies = []
        for entry, h in zip(() if direct else entries, held):
            copies.append([])
            for i, a in enumerate(entry):
                n = sum(len(c) for c in copies)
                to = h if len(entry) == 1 else h.at[:, pl.ds(a.shape[1] * i, a.shape[1])]
                copies[-1].append(pltpu.make_async_copy(sources[n], to, sem.at[n]))
                copies[-1][-1].start()
        here, leaving = set(range(len(entries)) if direct else ()), []

        def get(i):
            if i not in here:
                here.add(i)
                for copy in copies[i]:
                    copy.wait()
            return sources[i] if direct else held[i]

        def put(i, at=slice(None)):
            if keep:
                return
            copy = pltpu.make_async_copy(made[i].at[at], targets[i].at[at], out_sem.at[len(leaving)])
            copy.start()
            leaving.append(copy)
            whole.discard(i)

        whole = set(range(results))
        body(where_ref, get, put, *made)
        for i in sorted(whole):
            put(i)
        for i in range(len(entries)):
            get(i)
        for copy in leaving:
            copy.wait()

    shapes = [jax.ShapeDtypeStruct(shape, kind) for shape, kind in outs]
    return pl.pallas_call(
        inner,
        out_shape=shapes,
        in_specs=[pl.BlockSpec(memory_space=pltpu.SMEM)]
        + [pl.BlockSpec(memory_space=pltpu.VMEM if direct else pl.ANY)] * count
        + [pl.BlockSpec(memory_space=pl.ANY)] * len(after),
        out_specs=[pl.BlockSpec(memory_space=pltpu.VMEM if keep else pl.ANY)] * results,
        scratch_shapes=[pltpu.VMEM(shape_of(entry), entry[0].dtype) for entry in entries if not direct]
        + [pltpu.VMEM(a.shape, a.dtype) for a in shapes if not keep]
        + [pltpu.SemaphoreType.DMA((count,)), pltpu.SemaphoreType.DMA((most,))],
        compiler_params=pltpu.CompilerParams(vmem_limit_bytes=grant * 1024 * 1024),
        cost_estimate=pl.CostEstimate(flops=flops, bytes_accessed=size, transcendentals=0),
    )(where, *flat, *after)


def use_of(gate, count):
    slots = gate.shape[1]
    lane = lax.broadcasted_iota(jnp.int32, (1, slots), 1)
    use = jnp.where(lane < count, gate, 0.0)
    square = lax.broadcasted_iota(jnp.int32, (slots, slots), 0) == lax.broadcasted_iota(
        jnp.int32, (slots, slots), 1
    )
    return jnp.sum(jnp.where(square, use, 0.0), axis=1, keepdims=True)


def pick_of(token, tok):
    slots = token.shape[1]
    return jnp.where(lax.broadcasted_iota(jnp.int32, (tok, slots), 0) == token, 1.0, 0.0).astype(BF16)


def rows_body(where, get, put, own):
    token, count, gate, tokens = get(2), get(3), get(4), get(0)
    pick = pick_of(token[...], tokens.shape[0])
    own[0] = dot(pick, tokens[...], FIRST).astype(BF16)
    put(0, pl.ds(0, 1))
    own[1] = (use_of(gate[...], count[...]) * dot(pick, get(1)[...], FIRST)).astype(BF16)
    put(0, pl.ds(1, 1))


def turned_body(where, get, put, *turned):
    slots = get(0).shape[1]
    for step in range(N_X):
        for who in range(2):
            for which in range(2):
                turned[step][which, :, slots * who : slots * (who + 1)] = get(who * N_X + step)[which].T
        put(step)


def products_body(where, get, put, part, weights):
    pieces = get(0)
    rows, cols = pieces.shape[1] // 3, pieces.shape[2]
    for i in range(pieces.shape[0]):
        y, z = divmod(i, N_Z)
        place = y // 2 * 8 + z * 2 + y % 2
        for m in range(3):
            weights[place * rows : (place + 1) * rows, cols * m : cols * (m + 1)] = pieces[
                i, rows * m : rows * (m + 1)
            ]
    put(1)
    feat = get(1).shape[2]
    pre, back = 0.0, 0.0
    spans = [pl.ds(turn(where, step, feat), feat) for step in range(N_X)]
    for step, at in enumerate(spans):
        pre = pre + dot(get(1 + step)[0], weights[at, : 2 * cols])
    part[:, : 2 * cols] = pre.astype(BF16)
    put(0, (slice(None), pl.ds(0, 2 * cols)))
    for step, at in enumerate(spans):
        back = back + dot(get(1 + step)[1], weights[at, 2 * cols :])
    part[:, 2 * cols :] = back.astype(BF16)
    put(0, (slice(None), pl.ds(2 * cols, cols)))


def terms_body(where, get, put, pieces, acts, send):
    total = get(0)[...].astype(F32) + get(1)[...].astype(F32)
    units = total.shape[1] // 3
    pre_gate, pre_up, grad_hidden = total[:, :units], total[:, units : 2 * units], total[:, 2 * units :]
    sigma = jax.nn.sigmoid(pre_gate)
    acts[:, :units] = (
        grad_hidden * pre_up * sigma * (1.0 + pre_gate * (1.0 - sigma))
    ).astype(BF16)
    acts[:, units : 2 * units] = (grad_hidden * pre_gate * sigma).astype(BF16)
    acts[:, 2 * units :] = (pre_gate * sigma * pre_up).astype(BF16)
    send[...] = acts[send.shape[0] :]
    put(1)
    put(2)
    rows = pieces.shape[1] // 3
    for step in range(N_X):
        turned = get(2 + step)
        both = dot(turned[0], acts[:, : 2 * units]).astype(BF16)
        down = dot(turned[1], acts[:, 2 * units :]).astype(BF16)
        first = turn(where, step, 2 * N_Z)
        for i in range(2 * N_Z):
            y, z = divmod(i, N_Z)
            at = slice((z * 2 + y) * rows, (z * 2 + y + 1) * rows)
            pieces[first + i, :rows] = both[at, :units]
            pieces[first + i, rows : 2 * rows] = both[at, units:]
            pieces[first + i, 2 * rows :] = down[at]
        put(0, pl.ds(first, 2 * N_Z))


def outputs_body(where, get, put, *outs):
    slots, feat = outs[0].shape[1:]
    cols = get(1).shape[1] // 3
    for step in (2, 3, 1, 0):
        at = pl.ds(turn(where, step, feat), feat)
        out, back = 0.0, 0.0
        for who in range(2):
            acts, weights = get(2 * who), get(2 * who + 1)
            out = out + dot(acts[:slots, 2 * cols :], weights[at, 2 * cols :], LAST)
            back = back + dot(acts[:slots, : 2 * cols], weights[at, : 2 * cols], LAST)
        outs[step][0] = out.astype(BF16)
        outs[step][1] = back.astype(BF16)
        put(step)


def tokens_body(where, get, put, mixed, grad_tokens):
    token, count, gate = get(0), get(1), get(2)
    pick, use = pick_of(token[...], mixed.shape[0]), use_of(gate[...], count[...])
    out, back = [sum(get(3 + step)[i].astype(F32) for step in range(N_X)) for i in range(2)]
    mixed[...] = dot(pick, (use * out).astype(BF16)).astype(BF16)
    put(0)
    grad_tokens[...] = dot(pick, back.astype(BF16)).astype(BF16)


def local(tokens, grad_out, slot_token, slot_count, slot_gate, w_gate, w_up, w_down):
    slots, (tok, feat) = slot_token.shape[0], tokens.shape
    rows, cols = w_gate.shape
    token, gate, count = slot_token[None], slot_gate[None], slot_count[None]
    where = (lax.axis_index("narrow") // 2).astype(jnp.int32)[None]
    pick_flops = 4 * slots * tok * feat

    block = jnp.concatenate((w_gate, w_up, w_down), axis=0)
    block = lax.ppermute(block, ("wide", "narrow"), SWAP)
    (own,) = call(
        rows_body,
        [((2, slots, feat), BF16)],
        pick_flops,
        where,
        *(tokens, grad_out, token, count, gate),
    )
    block, own = lax.optimization_barrier((block, own))
    pieces = jnp.broadcast_to(block[None], (len(OWNERS[0]),) + block.shape)
    pieces = lax.all_to_all(pieces, "wide", 0, 0, axis_index_groups=OWNERS)
    near = {step: lax.ppermute(own, "narrow", shift_x(-step)) for step in (1, 3, 2)}
    near = [own] + [near[step] for step in range(1, N_X)]
    core = [lax.ppermute(held, "wide", OTHER_CORE) for held in near]
    turned = call(
        turned_body, [((2, feat, 2 * slots), BF16)] * N_X, TURN, where, *near, *core, grant=12, keep=True
    )

    flops = 2 * 3 * 2 * slots * N_X * feat * cols
    part = ((2 * slots, 3 * cols), BF16)
    sent, weights = call(
        products_body,
        [part, ((N_X * feat, 3 * cols), BF16)],
        flops,
        where,
        *(pieces, *([a, b] for a, b in zip(near, core))),
    )
    theirs = lax.ppermute(sent, "narrow", OTHER_HALF)
    core_weights = lax.ppermute(weights, "wide", OTHER_CORE)
    theirs, core_weights = lax.optimization_barrier((theirs, core_weights))
    terms, acts, send = call(
        terms_body,
        [(pieces.shape, BF16), part, ((slots, 3 * cols), BF16)],
        flops,
        where,
        *(sent, theirs, *turned),
        grant=12,
        direct=True,
    )


    terms = lax.all_to_all(terms, "wide", 0, 0, axis_index_groups=OWNERS)
    grads = terms.astype(F32).sum(axis=0).astype(BF16)
    grads = lax.ppermute(grads, ("wide", "narrow"), SWAP_BACK).astype(F32)

    got = lax.ppermute(send, "wide", OTHER_CORE)
    outs = call(
        outputs_body,
        [((2, slots, feat), BF16)] * N_X,
        flops,
        where,
        *(acts, weights, got, core_weights),
    )
    home = {step: lax.ppermute(outs[step], "narrow", shift_x(step)) for step in (1, 3, 2)}
    home = [outs[0]] + [home[step] for step in range(1, N_X)]
    mixed, grad_tokens = call(
        tokens_body,
        [((tok, feat), BF16)] * 2,
        pick_flops,
        where,
        *(token, count, gate, *home),
    )
    return mixed, grad_tokens, grads[:rows], grads[rows : 2 * rows], grads[2 * rows :]


def solution(mesh):
    both = P("wide", "narrow")
    in_specs = (both, both, P("wide"), P("wide"), P("wide"), both, both, both)
    return jax.shard_map(
        local, mesh=mesh, in_specs=in_specs, out_specs=(both,) * 5, check_vma=False
    )
```
